32 devices in a mesh: band: 4 (over y, core), tm: 8 (over z, x).
Axes of the slice: x: 2, y: 2, z: 4, core: 2. Of those that a mesh axis runs over, the one named last changes fastest.
Arguments:
- tod: bfloat16 [4, 64, 65536], P('band', None, 'tm'), may hold values from -6 to 6
- filter_taps: bfloat16 [4, 64, 2049], P('band'), may hold values from -0.125 to 0.125
- det_weights: float32 [4, 64], P('band'), may hold values from -0.75 to 0.75
- owner: int32 [4, 512, 1], P('band', 'tm'), may hold values from 0 to 7; in each aligned block of 64 rows (0 to 63, 64 to 127, ..., all dimensions but the last counted through in order) at most 32 rows name the same one
- tile_row: int32 [4, 512], P('band', 'tm'), may hold values from 0 to 127
- block_counts: int32 [4, 8], P('band', 'tm'), may hold values from 32 to 64, as said below
- beam_rows: float32 [4, 2, 33], P('band'), may hold values from -1 to 1
- beam_cols: float32 [4, 2, 33], P('band'), may hold values from -1 to 1
- mixing: float32 [4, 4, 2], P(None, 'band'), may hold values from -2 to 2
Outputs:
- components: float32 [4, 8, 128, 128], P(None, 'tm', 'band')
The draws below stay inside these ranges and needn't reach their ends.
Inputs may be any that keep to these rules, and one draw needn't show every extreme that they name: The owner of each scan block; among the 64 scan blocks of one time shard of one band at most 32 share an owner, and in every draw some time shard sends exactly 32 to one owner. A time shard keeps its first block_counts scan blocks, the rest carry nothing; the largest value is reached in every draw.
All inputs are finite; a program needn't handle non-finite values.
Results may differ from the reference program's by a relative error of at most 0.0003.
Values may be sent and summed in bfloat16 or wider, within the bound.
No kernel may reach another device: no remote copies, remote signals or barrier semaphores. Data moves between devices by JAX's collectives and lax.ppermute only.
A program may use at most 128 MiB of HBM per device.

```python
import math
import jax
import jax.numpy as jnp
import numpy as np
from jax import lax

DET = 64
TAPS = 2049
PIX = 128
TROWS = 128
BEAM = 33
NBEAM = 2
NCOMP = 4
BANDS = 4
BH = 16
NSAMP = 65536
NBLK = 64
NSB = 512
CAP = 32
MAPROWS = 1024
N_TM = 8


def draw_block_counts(key, part):
    shards = NSB // NBLK
    counts_drawn = jax.random.randint(key, (BANDS, shards), NBLK // 2, NBLK + 1)
    full_spot = jax.random.randint(jax.random.fold_in(key, 7), (), 0, BANDS * shards)
    counts_flat = counts_drawn.reshape(-1).at[full_spot].set(NBLK)
    return counts_flat.reshape(BANDS, shards).astype(jnp.int32)


def set_ends(entries, rng, least, top_value):
    longest = entries.shape.index(max(entries.shape))
    spots = []
    for shift in (0, 1):
        where = [jax.random.randint(jax.random.fold_in(rng, axis), (), 0, length) for axis, length in enumerate(entries.shape)]
        where[longest] = (where[longest] + shift) % entries.shape[longest]
        spots.append(tuple(where))
    return entries.at[spots[0]].set(least).at[spots[1]].set(top_value)


def levels(key, extent, cuts, smallest, high):
    loudness, own = 1.0, jax.random.fold_in(key, 6)
    for axis_at, blocks in cuts:
        draws = jnp.exp(jax.random.uniform(jax.random.fold_in(own, axis_at), (blocks,), jnp.float32, smallest / len(cuts), high / len(cuts)))
        loudness = loudness * jnp.repeat(draws, extent[axis_at] // blocks).reshape([-1 if axis == axis_at else 1 for axis in range(len(extent))])
    return loudness


def deal_out(key, own, number, rows, amount, top, most, skew):
    ranking = jax.random.permutation(key, amount)
    heavy_load, common = load_shares(amount, rows * top, most, skew, True), load_shares(amount, rows * top, most, skew, False)
    places = jnp.arange(amount)

    def named(sizes, rotation):
        used = int((sizes > 0).sum())
        fixed = max(1, used // 4)
        shifted = fixed + (places - fixed + rotation * (used - fixed)) % max(1, amount - fixed)
        return jnp.zeros((amount,), jnp.int32).at[ranking[jnp.where(places < fixed, places, shifted)]].set(jnp.asarray(sizes, jnp.int32))

    sizes = jnp.where(number % 4 == 0, named(heavy_load, number // 4), named(common, number - number // 4 - 1))
    mixed = jax.random.permutation(jax.random.fold_in(own, 3), amount)
    source_of, sink = mixed[0:amount // 2 * 2:2], mixed[1:amount // 2 * 2:2]
    margin = jnp.minimum(sizes[source_of] - 1, most - sizes[sink]) // 2
    margin = jnp.where((source_of == ranking[0]) | (sink == ranking[0]) | (sizes[sink] == 0), 0, jnp.maximum(margin, 0))
    shifted = jax.random.randint(jax.random.fold_in(own, 4), (amount // 2,), 0, 1 << 20) % (margin + 1)
    sizes = sizes.at[source_of].add(-shifted).at[sink].add(shifted)
    items = jnp.searchsorted(jnp.cumsum(sizes), jnp.arange(rows * top), side="right").astype(jnp.int32)
    listing = items.reshape(top, rows).T
    listing = listing[jax.random.permutation(jax.random.fold_in(own, 1), rows)]
    rotation = jax.random.randint(jax.random.fold_in(own, 2), (rows, 1), 0, top)
    return jnp.take_along_axis(listing, (jnp.arange(top)[None, :] + rotation) % top, axis=1)


def load_shares(number_of, total, reach, slope, full):
    weights = [(1 << 20) // math.isqrt(rank ** slope) + 1 for rank in range(1, number_of + 1)]
    largest = reach if full else min(reach, max(-(-total // number_of), total * weights[0] // sum(weights)))
    least = 1 if total - largest >= number_of - 1 else 0
    given, spare = [largest] + [least] * (number_of - 1), total - largest - least * (number_of - 1)
    while spare > 0:
        movable = [i for i in range(1, number_of) if given[i] < largest] or [i for i in range(1, number_of) if given[i] < reach]
        mass, remaining = sum([weights[i] for i in movable]), spare
        for i in movable:
            extra = min(reach - given[i], max(1, remaining * weights[i] // mass), spare)
            given[i] = given[i] + extra
            spare = spare - extra
    return np.array(given)


def normal_values(key, extent, spread, most, cuts=(), held_as=jnp.bfloat16):
    entries = jax.random.normal(key, extent, jnp.float32) * spread
    if len(cuts) > 0:
        entries = levels(key, extent, cuts, -0.22, 0.18) * entries
    return jnp.clip(entries, min=-most, max=most).astype(held_as)


def setup_inputs(seed: int = 0) -> dict:
    keys = jax.random.split(jax.random.key(seed), 10)
    tod = normal_values(keys[0], (BANDS, DET, NSAMP), 1.0, 6.0, ((0, 4), (2, 8)))
    filter_taps = normal_values(keys[1], (BANDS, DET, TAPS), TAPS ** -0.5, 0.125, ((0, 4),))
    det_weights = normal_values(keys[2], (BANDS, DET), DET ** -0.5, 0.75, ((0, 4),), jnp.float32)
    owner_keys = jax.random.split(jax.random.fold_in(keys[3], 1), BANDS * NSB // NBLK)
    owner_turns = jax.random.permutation(jax.random.fold_in(keys[3], 3), BANDS * NSB // NBLK)
    owner = jax.vmap(lambda own, number: deal_out(jax.random.fold_in(keys[3], 2), own, number, NBLK, N_TM, 1, CAP, 2))(owner_keys, owner_turns).reshape((BANDS, NSB, 1))
    tile_row = set_ends(jax.random.randint(keys[4], (BANDS, NSB), 0, TROWS), jax.random.fold_in(keys[4], 1), 0, TROWS - 1).astype(jnp.int32)
    block_counts = draw_block_counts(jax.random.fold_in(keys[9], 71), 0)
    beam_rows = normal_values(keys[6], (BANDS, NBEAM, BEAM), BEAM ** -0.5, 1.0, ((0, 4),), jnp.float32)
    beam_cols = normal_values(keys[7], (BANDS, NBEAM, BEAM), BEAM ** -0.5, 1.0, ((0, 4),), jnp.float32)
    mixing = normal_values(keys[8], (NCOMP, BANDS, NBEAM), (2 * BANDS) ** -0.5, 2.0, ((1, 4),), jnp.float32)
    return dict(tod=tod, filter_taps=filter_taps, det_weights=det_weights, owner=owner, tile_row=tile_row, block_counts=block_counts, beam_rows=beam_rows, beam_cols=beam_cols, mixing=mixing)


def toeplitz_rows(tap_row, seg_len):
    taps = tap_row.shape[0]
    width = seg_len + taps - 1
    padded_taps = jnp.concatenate([tap_row, jnp.zeros((seg_len,), tap_row.dtype)])
    tiled = jnp.tile(padded_taps, seg_len)[: seg_len * width]
    return tiled.reshape(seg_len, width)


def filter_group(group_args):
    padded_group, tap_group = group_args
    half_len = (tap_group.shape[1] - 1) // 2
    seg_len = math.gcd(half_len, 128)
    reach_pieces = 2 * half_len // seg_len
    group_size = padded_group.shape[0]
    segments = (padded_group.shape[1] - 2 * half_len) // seg_len
    pieces = padded_group.reshape(group_size, segments + reach_pieces, seg_len)
    windows = jnp.concatenate([pieces[:, shift:shift + segments] for shift in range(reach_pieces + 1)], axis=2)
    tables = jax.vmap(lambda tap_row: toeplitz_rows(tap_row, seg_len))(tap_group)
    product = lax.dot_general(windows.astype(jnp.float32), tables.astype(jnp.float32), (((2,), (2,)), ((0,), (0,))), precision=lax.Precision.HIGHEST, preferred_element_type=jnp.float32)
    return product.reshape(group_size, segments * seg_len)


def filter_band(tod_band, tap_rows):
    half_len = (tap_rows.shape[1] - 1) // 2
    detectors = tod_band.shape[0]
    samples = tod_band.shape[1]
    group_size = math.gcd(detectors, 16)
    padded = jnp.pad(tod_band, ((0, 0), (half_len, half_len)))
    padded = padded.reshape(detectors // group_size, group_size, samples + 2 * half_len)
    grouped_taps = tap_rows.reshape(detectors // group_size, group_size, tap_rows.shape[1])
    filtered = lax.map(filter_group, (padded, grouped_taps))
    return filtered.reshape(detectors, samples)


def reference(tod, filter_taps, det_weights, owner, tile_row, block_counts, beam_rows, beam_cols, mixing):
    def one_band(band_args):
        tod_band, tap_rows, weights, owners, pixel_rows, counts, row_profile, col_profile = band_args
        filtered = filter_band(tod_band, tap_rows)
        weighted = jnp.dot(weights, filtered, precision=lax.Precision.HIGHEST, preferred_element_type=jnp.float32)
        block_vals = weighted.reshape(NSB, PIX)
        block_index = jnp.arange(NSB, dtype=jnp.int32)
        local_index = block_index % NBLK
        shard_index = block_index // NBLK
        valid_mask = (local_index < counts[shard_index]).astype(jnp.float32)
        block_vals = block_vals * valid_mask[:, None]
        target = (owners[:, 0] * TROWS + pixel_rows).astype(jnp.int32)
        sky_map = jax.ops.segment_sum(block_vals, target, num_segments=MAPROWS)
        padded = jnp.pad(sky_map, ((BH, BH), (BH, BH)))
        results = []
        for beam in range(NBEAM):
            rowed = jnp.zeros((MAPROWS, PIX + 2 * BH), jnp.float32)
            for shift in range(BEAM):
                rowed = rowed + row_profile[beam, shift] * padded[shift:shift + MAPROWS, :]
            smoothed = jnp.zeros((MAPROWS, PIX), jnp.float32)
            for shift in range(BEAM):
                smoothed = smoothed + col_profile[beam, shift] * rowed[:, shift:shift + PIX]
            results.append(smoothed)
        return jnp.stack(results)

    beamed = lax.map(one_band, (tod, filter_taps, det_weights, owner, tile_row, block_counts, beam_rows, beam_cols))
    mixed = jnp.einsum("cbk,bkrp->crp", mixing, beamed, precision=lax.Precision.HIGHEST)
    return mixed.reshape(NCOMP, N_TM, TROWS, PIX)
```

```python
import functools

import jax
import jax.numpy as jnp
from jax import lax
from jax.experimental import pallas as pl
from jax.experimental.pallas import tpu as pltpu
from jax.sharding import PartitionSpec as P

L = 128
TROWS = 128
A = 8
R = 16
STEP = 64
GROUP = 704
UNROLL = 8
MARGIN = 8
VMEM = pl.BlockSpec(memory_space=pltpu.VMEM)
SMEM = pl.BlockSpec(memory_space=pltpu.SMEM)
PARAMS = pltpu.CompilerParams(vmem_limit_bytes=48 * 2**20)
F32, BF16 = jnp.float32, jnp.bfloat16


class Plan:
    def __init__(self, detectors, samples, taps):
        self.detectors, self.taps = detectors, taps
        self.shifts = L // STEP
        self.pieces = -(-(GROUP + STEP - 1) // L)
        self.groups = -(-taps // GROUP)
        self.blocks = samples // L
        self.lead = -(-((GROUP + STEP - 2) // STEP) // self.shifts)
        self.cols = -(-(self.blocks + self.lead) // A)
        self.reads = self.cols + self.pieces - 1
        self.stored = self.cols * (A - 1) + self.reads
        self.reach = (taps - 1) // 2 // L
        self.whole = (taps - 1) // L
        self.rows = self.shifts * self.cols * A
        self.width = STEP * self.groups
        self.lanes = -(-self.width // L)
        self.out = self.blocks + 2 * self.reach


def filter_kernel(
    weights, tod, taps, owner, tile_row, counts, out, shifted, tap_rows, table, acc, unmixed, line, *, plan
):
    nd, nb, lead = plan.detectors, plan.blocks, plan.lead
    lane_d = lax.broadcasted_iota(jnp.int32, (nd, L), 1)
    none = jnp.zeros((nd, L), BF16)

    def tile(g):
        return tod[0, :, g * L : (g + 1) * L] if 0 <= g < nb else none

    for q in range(plan.shifts):
        for i in range(plan.stored):
            g = i - lead
            piece = none
            if 0 <= g < nb or (q > 0 and g == -1):
                piece = tile(g)
                if q > 0:
                    piece = jnp.where(lane_d >= STEP * q, piece, tile(g + 1))
                    piece = pltpu.roll(piece, L - STEP * q, 1)
            shifted[q, i * nd : (i + 1) * nd, :] = piece.astype(F32)
    whole = plan.whole
    for i in range(whole):
        tap_rows[i * nd : (i + 1) * nd, :] = taps[0, :, i * L : (i + 1) * L].astype(F32)
    last = jnp.broadcast_to(taps[0, :, whole * L : whole * L + 1].astype(F32), (nd, L))
    tap_rows[whole * nd : (whole + 1) * nd, :] = jnp.where(lane_d == 0, last, 0.0)
    acc[...] = jnp.zeros_like(acc)
    table[...] = jnp.zeros_like(table)

    row8 = lax.broadcasted_iota(jnp.int32, (8, L), 0)
    lane8 = lax.broadcasted_iota(jnp.int32, (8, L), 1)
    row16 = lax.broadcasted_iota(jnp.int32, (R, L), 0)
    lane16 = lax.broadcasted_iota(jnp.int32, (R, L), 1)
    zero8 = jnp.zeros((8, L), F32)
    zero16 = jnp.zeros((R, L), BF16)

    def make_table(d, slot):
        low, high = [zero8], [zero8]
        for i in range(whole + 1):
            spread = jnp.broadcast_to(tap_rows[pl.ds(i * nd + d, 1), :], (8, L))
            low.append(pltpu.roll(spread, 0, 1, stride=1, stride_axis=0))
            high.append(pltpu.roll(spread, 8, 1, stride=1, stride_axis=0))
        base = {-1: zero16, whole + 1: zero16}
        for i in range(whole + 1):
            base[i] = jnp.concatenate(
                [
                    jnp.where(lane8 >= row8, low[i + 1], low[i]),
                    jnp.where(lane8 >= row8 + 8, high[i + 1], high[i]),
                ],
                axis=0,
            ).astype(BF16)
        for j in range(plan.groups):
            for g in range(STEP // R):
                for k in range(plan.pieces):
                    at = GROUP * j + L * k - R * g
                    i, r = at // L, at % L
                    if i > whole:
                        continue
                    piece = base[i]
                    if r:
                        piece = pltpu.roll(jnp.where(lane16 >= r, piece, base[i + 1]), L - r, 1)
                    if k == 0 and j > 0:
                        piece = jnp.where(lane16 >= row16 + R * g, piece, zero16)
                    if L * k + L + R * g > GROUP and j < plan.groups - 1:
                        piece = jnp.where(lane16 < row16 + (R * g + GROUP - L * k), piece, zero16)
                    table[slot, STEP * j + R * g : STEP * j + R * g + R, k * L : (k + 1) * L] = piece

    def apply_table(d, slot):
        rows = []
        for pair in range(plan.shifts // 2):
            reads = [
                jnp.concatenate(
                    [
                        shifted[2 * pair + side, pl.ds(c * nd + d, A, stride=plan.cols * nd), :]
                        for side in range(2)
                    ],
                    axis=0,
                ).astype(BF16)
                for c in range(plan.reads)
            ]
            for c in range(plan.cols):
                rows.append(jnp.concatenate(reads[c : c + plan.pieces], axis=1))
        windows = jnp.concatenate(rows, axis=0)
        product = lax.dot_general(
            windows, table[slot], (((1,), (1,)), ((), ())), preferred_element_type=F32
        )
        return product * weights[0, d]

    make_table(0, 0)

    def body(step, carry):
        total = None
        for k in range(UNROLL):
            d = UNROLL * step + k
            make_table(jnp.minimum(d + 1, nd - 1), (k + 1) % 2)
            part = apply_table(d, k % 2)
            total = part if total is None else total + part
        acc[...] += total
        return carry

    lax.fori_loop(0, nd // UNROLL, body, 0)

    span = plan.cols * A
    for pair in range(plan.shifts // 2):
        for c in range(plan.cols):
            for side in range(2):
                start = ((pair * plan.cols + c) * 2 + side) * A
                for v in range(plan.lanes):
                    wide = min(L, plan.width - v * L)
                    unmixed[v, pl.ds((2 * pair + side) * span + c, A, stride=plan.cols), 0:wide] = acc[
                        start : start + A, v * L : v * L + wide
                    ]
    line[...] = jnp.zeros_like(line)
    lanes = lax.broadcasted_iota(jnp.int32, (span, L), 1)
    for j in range(plan.groups):
        for q in range(plan.shifts):
            down, slot = divmod(q - (GROUP // STEP) * j, plan.shifts)
            v, start = divmod(STEP * j, L)
            part = unmixed[v, q * span : (q + 1) * span, :]
            turn = (STEP * slot - start) % L
            if turn:
                part = pltpu.roll(part, turn, 1)
            at = down - lead + 2 * plan.reach + MARGIN
            inside = (lanes >= STEP * slot) & (lanes < STEP * slot + STEP)
            line[at : at + span, :] += jnp.where(inside, part, 0.0)
    out[0 : plan.out, :] = line[MARGIN : MARGIN + plan.out, :]

    block = lax.broadcasted_iota(jnp.int32, (nb, L), 0)
    lane = lax.broadcasted_iota(jnp.int32, (nb, L), 1)
    owners = jnp.sum(jnp.where(block == lane, owner[0], 0), axis=0, keepdims=True)
    row = jnp.broadcast_to(jnp.pad(tile_row[...], ((0, 0), (0, L - nb))), (1, L))
    lane1 = lax.broadcasted_iota(jnp.int32, (1, L), 1)
    target = jnp.where(lane1 < counts[0, 0], owners * TROWS + row, -1)
    out[plan.out : plan.out + 8, :] = jnp.broadcast_to(target.astype(F32), (8, L))


def two_terms(x):
    high = x.astype(BF16)
    return high, (x - high.astype(F32)).astype(BF16)


def tile_kernel(
    near, far, beam_rows, beam_cols, mixing, out, marks, tile, *, plan, outer, inner, bands, reach
):
    part_rows = plan.out + 8
    me = lax.axis_index("tm")
    band = lax.axis_index("band")
    halo, nb = plan.reach, plan.blocks
    total = outer * inner
    marks[...] = jnp.full_like(marks, -1.0)
    parts = []
    for flip, ref in enumerate((near, far)[:inner]):
        for k in range(outer):
            t = jnp.bitwise_xor(me, k * inner + flip)
            parts.append((t, ref, k * part_rows))
            marks[pl.ds(8 + t, 1), :] = ref[k * part_rows + plan.out : k * part_rows + plan.out + 1, :]
    here = marks[8 : 8 + total, :]
    before = marks[7 : 7 + total, :]
    after = marks[9 : 9 + total, :]
    lane = lax.broadcasted_iota(jnp.int32, (total, L), 1)
    target = jnp.where(lane < halo, pltpu.roll(before, (halo - nb) % L, 1), pltpu.roll(here, halo, 1))
    target = jnp.where(lane >= halo + nb, pltpu.roll(after, halo + nb, 1), target)
    target = jnp.where(lane < plan.out, target, -1.0)
    marks[8 : 8 + total, :] = target
    ext = TROWS + 2 * reach
    first = (me * TROWS - reach).astype(F32)
    row = lax.broadcasted_iota(jnp.int32, (ext, L), 0).astype(F32) + first
    row = jnp.where(row < 0, -2.0, row)
    result = None
    for t, ref, start in parts:
        picks = (jnp.broadcast_to(marks[pl.ds(8 + t, 1), :], (ext, L)) == row).astype(F32)
        high, low = two_terms(ref[start : start + plan.out, :])
        both = jnp.concatenate([high, low], axis=1)
        got = jnp.dot(picks[:, : plan.out].astype(BF16), both, preferred_element_type=F32)
        result = got if result is None else result + got
    tile[...] = result[:, :L] + result[:, L:]
    share = TROWS // bands
    wide = 2 * share + 2 * reach
    mine = band // 2
    for h in range(bands // 2):
        pair = jnp.bitwise_xor(mine, h)
        start = pl.multiple_of(pair * (2 * share), 8)
        out[h, 0:wide, :] = tile[pl.ds(start, wide), :]
        taps = beam_rows.shape[2]
        for k in range(2):
            out[h, wide + k : wide + k + 1, :] = jnp.zeros((1, L), F32)
        out[h, wide : wide + 8, :] = jnp.zeros((8, L), F32)
        terms = beam_rows.shape[1]
        for k in range(terms):
            out[h, wide + k : wide + k + 1, 0:taps] = beam_rows[0, k : k + 1, :]
            out[h, wide + terms + k : wide + terms + k + 1, 0:taps] = beam_cols[0, k : k + 1, :]
        comps = mixing.shape[0]
        for c in range(comps):
            out[h, wide + 2 * terms + c // 4 : wide + 2 * terms + c // 4 + 1, 32 * (c % 4) : 32 * (c % 4) + terms] = mixing[
                c, 0:1, :
            ]


def dot3(a, b, dims):
    a0, a1 = two_terms(a)
    b0, b1 = two_terms(b)
    ka, kb = dims
    left = jnp.concatenate([a0, a0, a1], axis=ka)
    right = jnp.concatenate([b0, b1, b0], axis=kb)
    return lax.dot_general(left, right, (((ka,), (kb,)), ((), ())), preferred_element_type=F32)


def beam_kernel(*refs, share, reach, terms, comps, taps):
    ins, out = refs[:-1], refs[-1]
    core = lax.rem(lax.axis_index("band"), 2)
    wide = 2 * share + 2 * reach
    need = share + 2 * reach
    x = lax.broadcasted_iota(jnp.int32, (L, L), 0)
    c_in = lax.broadcasted_iota(jnp.int32, (L, L), 1)
    near = jnp.abs(c_in - x) <= reach
    totals = [None] * comps
    for ref in ins:
        for h in range(ref.shape[0]):
            rows = ref[h, pl.ds(pl.multiple_of(core * share, 8), need), :]
            mats = []
            for k in range(terms):
                spread = jnp.broadcast_to(ref[h, wide + k : wide + k + 1, :], (share, L))
                mats.append(pltpu.roll(spread, 0, 1, stride=1, stride_axis=0)[:, :need])
            rowed = dot3(jnp.concatenate(mats, axis=0), rows, (1, 0))
            for k in range(terms):
                at = wide + terms + k
                spread = jnp.broadcast_to(ref[h, at : at + 1, :], (L, L))
                cols = pltpu.roll(spread, L - reach, 1, stride=1, stride_axis=0)
                cols = jnp.where(near, cols, 0.0)
                beamed = dot3(rowed[k * share : (k + 1) * share], cols, (1, 1))
                for c in range(comps):
                    at = wide + 2 * terms + c // 4
                    mix = ref[h, at : at + 1, 32 * (c % 4) + k : 32 * (c % 4) + k + 1]
                    part = beamed * mix
                    totals[c] = part if totals[c] is None else totals[c] + part
    for c in range(comps):
        out[c, 0] = totals[c]


def flip(x, axis, bits):
    count = lax.axis_size(axis)
    return lax.ppermute(x, axis, [(i, i ^ bits) for i in range(count)])


def on_device(
    tod, filter_taps, det_weights, owner, tile_row, block_counts, beam_rows, beam_cols, mixing
):
    detectors, samples = tod.shape[1:]
    taps = filter_taps.shape[2]
    plan = Plan(detectors, samples, taps)
    tms, bands = lax.axis_size("tm"), lax.axis_size("band")
    inner = 2
    outer = tms // inner
    terms, beam = beam_rows.shape[1:]
    reach = (beam - 1) // 2
    comps = mixing.shape[0]
    span = plan.cols * A
    values = pl.pallas_call(
        functools.partial(filter_kernel, plan=plan),
        out_shape=jax.ShapeDtypeStruct((plan.out + 8, L), F32),
        in_specs=[SMEM, VMEM, VMEM, VMEM, VMEM, SMEM],
        out_specs=VMEM,
        scratch_shapes=[
            pltpu.VMEM((plan.shifts, plan.stored * detectors, L), F32),
            pltpu.VMEM(((plan.whole + 1) * detectors, L), F32),
            pltpu.VMEM((2, plan.width, plan.pieces * L), BF16),
            pltpu.VMEM((plan.rows, plan.width), F32),
            pltpu.VMEM((plan.lanes, plan.rows, L), F32),
            pltpu.VMEM((MARGIN + plan.out + plan.lead + 16 + plan.cols, L), F32),
        ],
        compiler_params=PARAMS,
        name="filter_blocks",
    )(det_weights, tod, filter_taps, owner, tile_row, block_counts)
    gathered = [values] + [flip(values, "tm", k * inner) for k in range(1, outer)]
    near = jnp.concatenate(gathered, axis=0)
    far = flip(near, "tm", 1)
    share = TROWS // bands
    wide = 2 * share + 2 * reach
    windows = pl.pallas_call(
        functools.partial(tile_kernel, plan=plan, outer=outer, inner=inner, bands=bands, reach=reach),
        out_shape=jax.ShapeDtypeStruct((bands // 2, wide + 8, L), F32),
        in_specs=[VMEM] * 5,
        out_specs=VMEM,
        scratch_shapes=[pltpu.VMEM((16 + tms, L), F32), pltpu.VMEM((TROWS + 2 * reach, L), F32)],
        compiler_params=PARAMS,
        name="gather_rows",
    )(near, far, beam_rows, beam_cols, mixing)
    own = windows[0:1]
    across = [flip(windows[h : h + 1], "band", 2 * h) for h in range(1, bands // 2)]
    mine = [own] + across
    other = [flip(m, "band", 1) for m in mine]
    return pl.pallas_call(
        functools.partial(beam_kernel, share=share, reach=reach, terms=terms, comps=comps, taps=beam),
        out_shape=jax.ShapeDtypeStruct((comps, 1, share, L), F32),
        in_specs=[VMEM] * (2 * len(mine)),
        out_specs=VMEM,
        compiler_params=PARAMS,
        name="smooth_and_mix",
    )(*mine, *other)


def solution(mesh):
    placed = (
        P("band", None, "tm"),
        P("band", None, None),
        P("band", None),
        P("band", "tm", None),
        P("band", "tm"),
        P("band", "tm"),
        P("band", None, None),
        P("band", None, None),
        P(None, "band", None),
    )
    return jax.shard_map(
        on_device,
        mesh=mesh,
        in_specs=placed,
        out_specs=P(None, "tm", "band", None),
        check_vma=False,
    )
```

```python
import functools

import jax
import jax.numpy as jnp
from jax import lax
from jax.experimental import pallas as pl
from jax.experimental.pallas import tpu as pltpu
from jax.sharding import PartitionSpec as P

L = 128
TROWS = 128
BLOCK = 256
VMEM = pl.BlockSpec(memory_space=pltpu.VMEM)
ANY = pl.BlockSpec(memory_space=pl.ANY)
SMALL = pltpu.CompilerParams(vmem_limit_bytes=32 * 2**20)
WHOLE = pltpu.CompilerParams(vmem_limit_bytes=60 * 2**20)
F32, BF16 = jnp.float32, jnp.bfloat16


class Plan:
    def __init__(self, detectors, samples, taps):
        self.detectors, self.samples, self.taps = detectors, samples, taps
        self.groups = (taps - 1) // BLOCK
        self.steps = samples // BLOCK
        self.lead = self.groups - 1
        self.blocks = samples // L
        self.reach = (taps - 1) // 2 // L
        self.out = self.blocks + 2 * self.reach


def filter_kernel(
    weights_in, tod, taps_in, owner_in, row_in, counts_in,
    out, weights, taps, owner, tile_row, counts, held, table, line, diagonal, sems, *, plan
):
    nd, steps, lead, groups = plan.detectors, plan.steps, plan.lead, plan.groups
    small = [
        pltpu.make_async_copy(src, dst, sems.at[steps + i])
        for i, (src, dst) in enumerate(
            ((taps_in.at[0], taps), (weights_in, weights), (owner_in.at[0], owner), (row_in, tile_row), (counts_in, counts))
        )
    ]
    big = [
        pltpu.make_async_copy(
            tod.at[0, :, b * BLOCK : (b + 1) * BLOCK], held.at[(lead + b) * nd : (lead + b + 1) * nd, :], sems.at[b]
        )
        for b in range(steps)
    ]
    for copy in small + big:
        copy.start()
    held[0 : lead * nd, :] = jnp.zeros((lead * nd, BLOCK), BF16)
    held[(lead + steps) * nd :, :] = jnp.zeros((lead * nd, BLOCK), BF16)
    line[...] = jnp.zeros_like(line)
    row = lax.broadcasted_iota(jnp.int32, (nd, L), 0)
    lane = lax.broadcasted_iota(jnp.int32, (nd, L), 1)
    for copy in small:
        copy.wait()
    spread = jnp.broadcast_to(jnp.pad(weights[...], ((0, 0), (0, L - nd))), (nd, L))
    column = jnp.sum(jnp.where(row == lane, spread, 0.0), axis=1, keepdims=True)
    for pair in range(groups // 2):
        for half in range(2):
            parts = []
            for j in (2 * pair, 2 * pair + 1):
                start = j * BLOCK + half * L
                part = taps[:, start : start + L].astype(F32) * column
                parts.append(jnp.take_along_axis(part, L - 1 - lane, axis=1))
            turned = jnp.concatenate(parts, axis=0).T
            high, low = two_terms(turned)
            at = (1 - half) * L
            table[at : at + L, pair * L : (pair + 1) * L] = high
            table[BLOCK + at : BLOCK + at + L, pair * L : (pair + 1) * L] = low
    last = jnp.broadcast_to(taps[:, groups * BLOCK : groups * BLOCK + 1].astype(F32) * column, (nd, L))
    row8 = lax.broadcasted_iota(jnp.int32, (8, L), 0)
    lane8 = lax.broadcasted_iota(jnp.int32, (8, L), 1)
    for copy in big:
        copy.wait()

    slots = diagonal.shape[0]
    count = steps + lead

    def product(v):
        x = held[v * nd : (v + groups) * nd, :]
        both = jnp.dot(table[...], x, preferred_element_type=F32)
        diagonal[v % slots] = both[:BLOCK] + both[BLOCK:]

    def add_diagonals(tiles, at):
        total = direct = None
        for b in range(0, L, 8):
            part = tiles[0][b : b + 8]
            for other in tiles[1:]:
                part += other[b : b + 8]
            part = pltpu.roll(part, b + 1, 1, stride=1, stride_axis=0)
            kept = jnp.where(lane8 > row8 + b, part, 0.0)
            total = part if total is None else total + part
            direct = kept if direct is None else direct + kept
        line[at] += direct
        line[at + 1] += total - direct

    def corner(v, down, across):
        return diagonal[v % slots, down * L : (down + 1) * L, across * L : (across + 1) * L]

    product(0)
    for v in range(count):
        if v + 1 < count:
            product(v + 1)
        first = [corner(v, 0, 0)] + ([corner(v - 1, 1, 1)] if v else [])
        add_diagonals(first, 2 * v)
        add_diagonals([corner(v, 1, 0), corner(v, 0, 1)], 2 * v + 1)
        if v >= lead:
            for half in range(2):
                x = held[v * nd : (v + 1) * nd, half * L : (half + 1) * L]
                line[2 * (v - lead) + half] += (x.astype(F32) * last).reshape(nd // 8, 8, L).sum(0)
    add_diagonals([corner(count - 1, 1, 1)], 2 * count)
    out[0 : plan.out, :] = jnp.sum(line[0 : plan.out], axis=1)

    nb = plan.blocks
    row = lax.broadcasted_iota(jnp.int32, (nb, L), 0)
    lane = lax.broadcasted_iota(jnp.int32, (nb, L), 1)
    owners = jnp.sum(jnp.where(row == lane, owner[...], 0), axis=0, keepdims=True)
    rows = jnp.pad(tile_row[...], ((0, 0), (0, L - nb)))
    target = jnp.where(lane[:1] < counts[0, 0], owners * TROWS + rows, -1)
    out[plan.out : plan.out + 8, :] = jnp.broadcast_to(target.astype(F32), (8, L))


def two_terms(x):
    high = x.astype(BF16)
    return high, (x - high.astype(F32)).astype(BF16)


def tile_kernel(
    near, far, beam_rows, beam_cols, mixing, out, marks, tile, *, plan, outer, inner, bands, reach
):
    part_rows = plan.out + 8
    me = lax.axis_index("tm")
    band = lax.axis_index("band")
    halo, nb = plan.reach, plan.blocks
    total = outer * inner
    marks[...] = jnp.full_like(marks, -1.0)
    parts = []
    for flip, ref in enumerate((near, far)[:inner]):
        for k in range(outer):
            t = jnp.bitwise_xor(me, k * inner + flip)
            parts.append((t, ref, k * part_rows))
            marks[pl.ds(8 + t, 1), :] = ref[k * part_rows + plan.out : k * part_rows + plan.out + 1, :]
    here = marks[8 : 8 + total, :]
    before = marks[7 : 7 + total, :]
    after = marks[9 : 9 + total, :]
    lane = lax.broadcasted_iota(jnp.int32, (total, L), 1)
    target = jnp.where(lane < halo, pltpu.roll(before, (halo - nb) % L, 1), pltpu.roll(here, halo, 1))
    target = jnp.where(lane >= halo + nb, pltpu.roll(after, halo + nb, 1), target)
    target = jnp.where(lane < plan.out, target, -1.0)
    marks[8 : 8 + total, :] = target
    ext = TROWS + 2 * reach
    first = (me * TROWS - reach).astype(F32)
    row = lax.broadcasted_iota(jnp.int32, (ext, L), 0).astype(F32) + first
    row = jnp.where(row < 0, -2.0, row)
    result = None
    for t, ref, start in parts:
        picks = (jnp.broadcast_to(marks[pl.ds(8 + t, 1), :], (ext, L)) == row).astype(F32)
        high, low = two_terms(ref[start : start + plan.out, :])
        both = jnp.concatenate([high, low], axis=1)
        got = jnp.dot(picks[:, : plan.out].astype(BF16), both, preferred_element_type=F32)
        result = got if result is None else result + got
    tile[...] = result[:, :L] + result[:, L:]
    share = TROWS // bands
    wide = 2 * share + 2 * reach
    mine = band // 2
    for h in range(bands // 2):
        pair = jnp.bitwise_xor(mine, h)
        start = pl.multiple_of(pair * (2 * share), 8)
        out[h, 0:wide, :] = tile[pl.ds(start, wide), :]
        taps = beam_rows.shape[2]
        for k in range(2):
            out[h, wide + k : wide + k + 1, :] = jnp.zeros((1, L), F32)
        out[h, wide : wide + 8, :] = jnp.zeros((8, L), F32)
        terms = beam_rows.shape[1]
        for k in range(terms):
            out[h, wide + k : wide + k + 1, 0:taps] = beam_rows[0, k : k + 1, :]
            out[h, wide + terms + k : wide + terms + k + 1, 0:taps] = beam_cols[0, k : k + 1, :]
        comps = mixing.shape[0]
        for c in range(comps):
            out[h, wide + 2 * terms + c // 4 : wide + 2 * terms + c // 4 + 1, 32 * (c % 4) : 32 * (c % 4) + terms] = mixing[
                c, 0:1, :
            ]


def dot3(a, b, dims):
    a0, a1 = two_terms(a)
    b0, b1 = two_terms(b)
    ka, kb = dims
    left = jnp.concatenate([a0, a0, a1], axis=ka)
    right = jnp.concatenate([b0, b1, b0], axis=kb)
    return lax.dot_general(left, right, (((ka,), (kb,)), ((), ())), preferred_element_type=F32)


def beam_kernel(*refs, share, reach, terms, comps, taps):
    ins, out = refs[:-1], refs[-1]
    core = lax.rem(lax.axis_index("band"), 2)
    wide = 2 * share + 2 * reach
    need = share + 2 * reach
    x = lax.broadcasted_iota(jnp.int32, (L, L), 0)
    c_in = lax.broadcasted_iota(jnp.int32, (L, L), 1)
    near = jnp.abs(c_in - x) <= reach
    totals = [None] * comps
    for ref in ins:
        for h in range(ref.shape[0]):
            rows = ref[h, pl.ds(pl.multiple_of(core * share, 8), need), :]
            mats = []
            for k in range(terms):
                spread = jnp.broadcast_to(ref[h, wide + k : wide + k + 1, :], (share, L))
                mats.append(pltpu.roll(spread, 0, 1, stride=1, stride_axis=0)[:, :need])
            rowed = dot3(jnp.concatenate(mats, axis=0), rows, (1, 0))
            for k in range(terms):
                at = wide + terms + k
                spread = jnp.broadcast_to(ref[h, at : at + 1, :], (L, L))
                cols = pltpu.roll(spread, L - reach, 1, stride=1, stride_axis=0)
                cols = jnp.where(near, cols, 0.0)
                beamed = dot3(rowed[k * share : (k + 1) * share], cols, (1, 1))
                for c in range(comps):
                    at = wide + 2 * terms + c // 4
                    mix = ref[h, at : at + 1, 32 * (c % 4) + k : 32 * (c % 4) + k + 1]
                    part = beamed * mix
                    totals[c] = part if totals[c] is None else totals[c] + part
    for c in range(comps):
        out[c, 0] = totals[c]


def flip(x, axis, bits):
    count = lax.axis_size(axis)
    return lax.ppermute(x, axis, [(i, i ^ bits) for i in range(count)])


def on_device(
    tod, filter_taps, det_weights, owner, tile_row, block_counts, beam_rows, beam_cols, mixing
):
    detectors, samples = tod.shape[1:]
    taps = filter_taps.shape[2]
    plan = Plan(detectors, samples, taps)
    tms, bands = lax.axis_size("tm"), lax.axis_size("band")
    inner = 2
    outer = tms // inner
    terms, beam = beam_rows.shape[1:]
    reach = (beam - 1) // 2
    comps = mixing.shape[0]
    values = pl.pallas_call(
        functools.partial(filter_kernel, plan=plan),
        out_shape=jax.ShapeDtypeStruct((plan.out + 8, L), F32),
        in_specs=[ANY] * 6,
        out_specs=VMEM,
        scratch_shapes=[
            pltpu.VMEM((1, detectors), F32),
            pltpu.VMEM((detectors, taps), BF16),
            pltpu.VMEM((plan.blocks, 1), jnp.int32),
            pltpu.VMEM((1, plan.blocks), jnp.int32),
            pltpu.SMEM((1, 1), jnp.int32),
            pltpu.VMEM(((plan.steps + 2 * plan.lead) * detectors, BLOCK), BF16),
            pltpu.VMEM((2 * BLOCK, plan.groups * detectors), BF16),
            pltpu.VMEM((plan.out + 8, 8, L), F32),
            pltpu.VMEM((3, BLOCK, BLOCK), F32),
            pltpu.SemaphoreType.DMA((plan.steps + 5,)),
        ],
        compiler_params=WHOLE,
        name="filter_blocks",
    )(det_weights, tod, filter_taps, owner, tile_row, block_counts)
    gathered = [values] + [flip(values, "tm", k * inner) for k in range(1, outer)]
    near = jnp.concatenate(gathered, axis=0)
    far = flip(near, "tm", 1)
    share = TROWS // bands
    wide = 2 * share + 2 * reach
    windows = pl.pallas_call(
        functools.partial(tile_kernel, plan=plan, outer=outer, inner=inner, bands=bands, reach=reach),
        out_shape=jax.ShapeDtypeStruct((bands // 2, wide + 8, L), F32),
        in_specs=[VMEM] * 5,
        out_specs=VMEM,
        scratch_shapes=[pltpu.VMEM((16 + tms, L), F32), pltpu.VMEM((TROWS + 2 * reach, L), F32)],
        compiler_params=SMALL,
        name="gather_rows",
    )(near, far, beam_rows, beam_cols, mixing)
    own = windows[0:1]
    across = [flip(windows[h : h + 1], "band", 2 * h) for h in range(1, bands // 2)]
    mine = [own] + across
    other = [flip(m, "band", 1) for m in mine]
    return pl.pallas_call(
        functools.partial(beam_kernel, share=share, reach=reach, terms=terms, comps=comps, taps=beam),
        out_shape=jax.ShapeDtypeStruct((comps, 1, share, L), F32),
        in_specs=[VMEM] * (2 * len(mine)),
        out_specs=VMEM,
        compiler_params=SMALL,
        name="smooth_and_mix",
    )(*mine, *other)


def solution(mesh):
    placed = (
        P("band", None, "tm"),
        P("band", None, None),
        P("band", None),
        P("band", "tm", None),
        P("band", "tm"),
        P("band", "tm"),
        P("band", None, None),
        P("band", None, None),
        P(None, "band", None),
    )
    return jax.shard_map(
        on_device,
        mesh=mesh,
        in_specs=placed,
        out_specs=P(None, "tm", "band", None),
        check_vma=False,
    )
```

```python
import functools

import jax
import jax.numpy as jnp
from jax import lax
from jax.experimental import pallas as pl
from jax.experimental.pallas import tpu as pltpu
from jax.sharding import PartitionSpec as P

L = 128
TROWS = 128
BLOCK = 256
VMEM = pl.BlockSpec(memory_space=pltpu.VMEM)
ANY = pl.BlockSpec(memory_space=pl.ANY)
SMALL = pltpu.CompilerParams(vmem_limit_bytes=32 * 2**20)
WHOLE = pltpu.CompilerParams(vmem_limit_bytes=60 * 2**20)
F32, BF16 = jnp.float32, jnp.bfloat16


class Plan:
    def __init__(self, detectors, samples, taps):
        self.detectors, self.samples, self.taps = detectors, samples, taps
        self.groups = (taps - 1) // BLOCK
        self.steps = samples // BLOCK
        self.lead = self.groups - 1
        self.blocks = samples // L
        self.reach = (taps - 1) // 2 // L
        self.out = self.blocks + 2 * self.reach


def filter_kernel(
    weights_in, tod, taps_in, owner_in, row_in, counts_in,
    out, weights, taps, owner, tile_row, counts, held, table, line, diagonal, sems, *, plan
):
    nd, steps, lead, groups = plan.detectors, plan.steps, plan.lead, plan.groups
    small = [
        pltpu.make_async_copy(src, dst, sems.at[steps + i])
        for i, (src, dst) in enumerate(
            ((taps_in.at[0], taps), (weights_in, weights), (owner_in, owner), (row_in, tile_row), (counts_in, counts))
        )
    ]
    big = [
        pltpu.make_async_copy(
            tod.at[0, :, b * BLOCK : (b + 1) * BLOCK], held.at[(lead + b) * nd : (lead + b + 1) * nd, :], sems.at[b]
        )
        for b in range(steps)
    ]
    for copy in small + big:
        copy.start()
    held[0 : lead * nd, :] = jnp.zeros((lead * nd, BLOCK), BF16)
    held[(lead + steps) * nd :, :] = jnp.zeros((lead * nd, BLOCK), BF16)
    line[...] = jnp.zeros_like(line)
    row = lax.broadcasted_iota(jnp.int32, (nd, L), 0)
    lane = lax.broadcasted_iota(jnp.int32, (nd, L), 1)
    for copy in small:
        copy.wait()
    spread = jnp.broadcast_to(jnp.pad(weights[...], ((0, 0), (0, L - nd))), (nd, L))
    column = jnp.sum(jnp.where(row == lane, spread, 0.0), axis=1, keepdims=True)
    for pair in range(groups // 2):
        for half in range(2):
            parts = []
            for j in (2 * pair, 2 * pair + 1):
                start = j * BLOCK + half * L
                part = taps[:, start : start + L].astype(F32) * column
                parts.append(jnp.take_along_axis(part, L - 1 - lane, axis=1))
            turned = jnp.concatenate(parts, axis=0).T
            high, low = two_terms(turned)
            at = (1 - half) * L
            table[at : at + L, pair * L : (pair + 1) * L] = high
            table[BLOCK + at : BLOCK + at + L, pair * L : (pair + 1) * L] = low
    last = jnp.broadcast_to(taps[:, groups * BLOCK : groups * BLOCK + 1].astype(F32) * column, (nd, L))
    row8 = lax.broadcasted_iota(jnp.int32, (8, L), 0)
    lane8 = lax.broadcasted_iota(jnp.int32, (8, L), 1)
    for copy in big:
        copy.wait()

    slots = diagonal.shape[0]
    count = steps + lead

    def product(v):
        half = groups // 2
        low = half if v + half <= lead else 0
        high = half if v + half >= lead + steps else groups
        x = held[(v + low) * nd : (v + high) * nd, :]
        both = jnp.dot(table[:, low * nd : high * nd], x, preferred_element_type=F32)
        diagonal[v % slots] = both[:BLOCK] + both[BLOCK:]

    def add_diagonals(tiles, at):
        total = direct = None
        for b in range(0, L, 8):
            part = tiles[0][b : b + 8]
            for other in tiles[1:]:
                part += other[b : b + 8]
            part = pltpu.roll(part, b + 1, 1, stride=1, stride_axis=0)
            kept = jnp.where(lane8 > row8 + b, part, 0.0)
            total = part if total is None else total + part
            direct = kept if direct is None else direct + kept
        line[at] += direct
        line[at + 1] += total - direct

    def corner(v, down, across):
        return diagonal[v % slots, down * L : (down + 1) * L, across * L : (across + 1) * L]

    product(0)
    for v in range(count):
        if v + 1 < count:
            product(v + 1)
        first = [corner(v, 0, 0)] + ([corner(v - 1, 1, 1)] if v else [])
        add_diagonals(first, 2 * v)
        add_diagonals([corner(v, 1, 0), corner(v, 0, 1)], 2 * v + 1)
        if v >= lead:
            for half in range(2):
                x = held[v * nd : (v + 1) * nd, half * L : (half + 1) * L]
                line[2 * (v - lead) + half] += (x.astype(F32) * last).reshape(nd // 8, 8, L).sum(0)
    add_diagonals([corner(count - 1, 1, 1)], 2 * count)
    out[0 : plan.out, :] = jnp.sum(line[0 : plan.out], axis=1)

    nb = plan.blocks
    pad = ((0, 0), (0, L - nb))
    target = jnp.pad(owner[...], pad) * TROWS + jnp.pad(tile_row[...], pad)
    kept = lax.broadcasted_iota(jnp.int32, (1, L), 1) < counts[0, 0]
    target = jnp.where(kept, target, -1)
    out[plan.out : plan.out + 8, :] = jnp.broadcast_to(target.astype(F32), (8, L))


def two_terms(x):
    high = x.astype(BF16)
    return high, (x - high.astype(F32)).astype(BF16)


def rows_of(target, first, count):
    row = lax.broadcasted_iota(jnp.int32, (count, target.shape[1]), 0).astype(F32) + first
    row = jnp.where(row < 0, -2.0, row)
    return (jnp.broadcast_to(target, row.shape) == row).astype(BF16)


def add_rows(picks, blocks):
    high, low = two_terms(blocks)
    both = jnp.dot(picks, jnp.concatenate([high, low], axis=1), preferred_element_type=F32)
    return both[:, :L] + both[:, L:]


def tile_rows_kernel(*refs, plan, reach):
    parts, (home, away) = refs[:-2], refs[-2:]
    nb, halo = plan.blocks, plan.reach
    me = lax.axis_index("tm")
    ext = TROWS + 2 * reach
    target = jnp.concatenate([ref[plan.out : plan.out + 1, 0:nb] for ref in parts], axis=1)
    blocks = jnp.concatenate([ref[halo : halo + nb, :] for ref in parts], axis=0)
    for out, tile in ((home, me), (away, jnp.bitwise_xor(me, 1))):
        picks = rows_of(target, (tile * TROWS - reach).astype(F32), ext)
        out[0:ext, :] = add_rows(picks, blocks)
    for k, ref in enumerate(parts):
        at = ext + 2 * halo * k
        away[at : at + halo, :] = ref[0:halo, :]
        away[at + halo : at + 2 * halo, :] = ref[halo + nb : plan.out, :]
    at = ext + 2 * halo * len(parts)
    away[at:, :] = jnp.full((away.shape[0] - at, L), -1.0, F32)
    for k, ref in enumerate(parts):
        away[at + k : at + k + 1, :] = ref[plan.out : plan.out + 1, :]


def windows_kernel(*refs, plan, outer, bands, reach):
    parts = refs[:outer]
    home, other, beam_rows, beam_cols, mixing, out, marks, tile = refs[outer:]
    me = lax.axis_index("tm")
    mine = lax.axis_index("band") // 2
    nb, halo = plan.blocks, plan.reach
    ext = TROWS + 2 * reach
    after_rows = ext + 2 * halo * outer
    marks[...] = jnp.full_like(marks, -1.0)
    numbers = []
    for k, ref in enumerate(parts):
        t = jnp.bitwise_xor(me, 2 * k)
        marks[pl.ds(8 + t, 1), :] = ref[plan.out : plan.out + 1, :]
        numbers.append(t)
    for k in range(outer):
        t = jnp.bitwise_xor(me, 2 * k + 1)
        marks[pl.ds(8 + t, 1), :] = other[after_rows + k : after_rows + k + 1, :]
        numbers.append(t)
    targets = []
    for t in numbers:
        before = marks[pl.ds(7 + t, 1), :]
        after = marks[pl.ds(9 + t, 1), :]
        targets += [before[:, nb - halo : nb], after[:, 0:halo]]
    blocks = []
    for ref in parts:
        blocks += [ref[0:halo, :], ref[halo + nb : plan.out, :]]
    blocks.append(other[ext:after_rows, :])
    picks = rows_of(jnp.concatenate(targets, axis=1), (me * TROWS - reach).astype(F32), ext)
    tile[...] = home[...] + other[0:ext, :] + add_rows(picks, jnp.concatenate(blocks, axis=0))
    share = TROWS // bands
    wide = 2 * share + 2 * reach
    terms, taps = beam_rows.shape[1:]
    comps = mixing.shape[0]
    out[...] = jnp.zeros_like(out)
    pad = jnp.zeros((8, L - taps), F32)
    lane = lax.broadcasted_iota(jnp.int32, (8, L), 1)
    turn = jnp.where(lane < taps, taps - 1 - lane, lane)
    for h in range(bands // 2):
        start = pl.multiple_of(jnp.bitwise_xor(mine, h) * (2 * share), 8)
        out[h, 0:wide, :] = tile[pl.ds(start, wide), :]
        for k in range(terms):
            out[h, wide + k : wide + k + 1, 0:taps] = beam_rows[0, k : k + 1, :]
            profile = jnp.broadcast_to(beam_cols[0, k : k + 1, :], (8, taps))
            turned = jnp.take_along_axis(jnp.concatenate([profile, pad], axis=1), turn, axis=1)
            out[h, wide + terms + k : wide + terms + k + 1, :] = turned[0:1]
            for c in range(comps):
                at = wide + 2 * terms + c * terms + k
                out[h, at : at + 1, :] = jnp.broadcast_to(mixing[c, 0:1, k : k + 1], (1, L))


def dot3(a, b, dims):
    a0, a1 = two_terms(a)
    b0, b1 = two_terms(b)
    ka, kb = dims
    left = jnp.concatenate([a0, a0, a1], axis=ka)
    right = jnp.concatenate([b0, b1, b0], axis=kb)
    return lax.dot_general(left, right, (((ka,), (kb,)), ((), ())), preferred_element_type=F32)


def beam_kernel(*refs, share, reach, terms, comps, taps):
    ins, out = refs[:-1], refs[-1]
    core = lax.rem(lax.axis_index("band"), 2)
    wide = 2 * share + 2 * reach
    need = share + 2 * reach
    x = lax.broadcasted_iota(jnp.int32, (L, L), 0)
    c_in = lax.broadcasted_iota(jnp.int32, (L, L), 1)
    near = jnp.abs(c_in - x) <= reach
    totals = [None] * comps
    for ref in ins:
        for h in range(ref.shape[0]):
            rows = ref[h, pl.ds(pl.multiple_of(core * share, 8), need), :]
            mats = []
            for k in range(terms):
                spread = jnp.broadcast_to(ref[h, wide + k : wide + k + 1, :], (share, L))
                mats.append(pltpu.roll(spread, 0, 1, stride=1, stride_axis=0)[:, :need])
            rowed = dot3(jnp.concatenate(mats, axis=0), rows, (1, 0))
            for k in range(terms):
                at = wide + terms + k
                spread = jnp.broadcast_to(ref[h, at : at + 1, :], (L, L))
                cols = pltpu.roll(spread, L - reach, 1, stride=1, stride_axis=0)
                cols = jnp.where(near, cols, 0.0)
                beamed = dot3(rowed[k * share : (k + 1) * share], cols, (1, 0))
                for c in range(comps):
                    at = wide + 2 * terms + c * terms + k
                    part = beamed * ref[h, at : at + 1, :]
                    totals[c] = part if totals[c] is None else totals[c] + part
    for c in range(comps):
        out[c, 0] = totals[c]


def flip(x, axis, bits):
    count = lax.axis_size(axis)
    return lax.ppermute(x, axis, [(i, i ^ bits) for i in range(count)])


def on_device(
    tod, filter_taps, det_weights, owner, tile_row, block_counts, beam_rows, beam_cols, mixing
):
    detectors, samples = tod.shape[1:]
    taps = filter_taps.shape[2]
    plan = Plan(detectors, samples, taps)
    tms, bands = lax.axis_size("tm"), lax.axis_size("band")
    inner = 2
    outer = tms // inner
    terms, beam = beam_rows.shape[1:]
    reach = (beam - 1) // 2
    comps = mixing.shape[0]
    values = pl.pallas_call(
        functools.partial(filter_kernel, plan=plan),
        out_shape=jax.ShapeDtypeStruct((plan.out + 8, L), F32),
        in_specs=[ANY] * 6,
        out_specs=VMEM,
        scratch_shapes=[
            pltpu.VMEM((1, detectors), F32),
            pltpu.VMEM((detectors, taps), BF16),
            pltpu.VMEM((1, plan.blocks), jnp.int32),
            pltpu.VMEM((1, plan.blocks), jnp.int32),
            pltpu.SMEM((1, 1), jnp.int32),
            pltpu.VMEM(((plan.steps + 2 * plan.lead) * detectors, BLOCK), BF16),
            pltpu.VMEM((2 * BLOCK, plan.groups * detectors), BF16),
            pltpu.VMEM((plan.out + 8, 8, L), F32),
            pltpu.VMEM((3, BLOCK, BLOCK), F32),
            pltpu.SemaphoreType.DMA((plan.steps + 5,)),
        ],
        compiler_params=WHOLE,
        name="filter_blocks",
    )(det_weights, tod, filter_taps, owner[:, :, 0], tile_row, block_counts)
    parts = [values] + [flip(values, "tm", k * inner) for k in range(1, outer)]
    ext = TROWS + 2 * reach
    sent = ext + 2 * plan.reach * outer + -(-outer // 8) * 8
    home, away = pl.pallas_call(
        functools.partial(tile_rows_kernel, plan=plan, reach=reach),
        out_shape=(jax.ShapeDtypeStruct((ext, L), F32), jax.ShapeDtypeStruct((sent, L), F32)),
        in_specs=[VMEM] * outer,
        out_specs=(VMEM, VMEM),
        compiler_params=SMALL,
        name="tile_rows",
    )(*parts)
    other = flip(away, "tm", 1)
    share = TROWS // bands
    wide = 2 * share + 2 * reach
    extra = -(-(2 * terms + comps * terms) // 8) * 8
    windows = pl.pallas_call(
        functools.partial(windows_kernel, plan=plan, outer=outer, bands=bands, reach=reach),
        out_shape=jax.ShapeDtypeStruct((bands // 2, wide + extra, L), F32),
        in_specs=[VMEM] * (outer + 5),
        out_specs=VMEM,
        scratch_shapes=[pltpu.VMEM((16 + tms, L), F32), pltpu.VMEM((ext, L), F32)],
        compiler_params=SMALL,
        name="band_windows",
    )(*parts, home, other, beam_rows, beam_cols, mixing)
    own = windows[0:1]
    across = [flip(windows[h : h + 1], "band", 2 * h) for h in range(1, bands // 2)]
    mine = [own] + across
    other = [flip(m, "band", 1) for m in mine]
    return pl.pallas_call(
        functools.partial(beam_kernel, share=share, reach=reach, terms=terms, comps=comps, taps=beam),
        out_shape=jax.ShapeDtypeStruct((comps, 1, share, L), F32),
        in_specs=[VMEM] * (2 * len(mine)),
        out_specs=VMEM,
        compiler_params=SMALL,
        name="smooth_and_mix",
    )(*mine, *other)


def solution(mesh):
    placed = (
        P("band", None, "tm"),
        P("band", None, None),
        P("band", None),
        P("band", "tm", None),
        P("band", "tm"),
        P("band", "tm"),
        P("band", None, None),
        P("band", None, None),
        P(None, "band", None),
    )
    return jax.shard_map(
        on_device,
        mesh=mesh,
        in_specs=placed,
        out_specs=P(None, "tm", "band", None),
        check_vma=False,
    )
```

```python
import functools

import jax
import jax.numpy as jnp
from jax import lax
from jax.experimental import pallas as pl
from jax.experimental.pallas import tpu as pltpu
from jax.sharding import PartitionSpec as P

L = 128
TROWS = 128
BLOCK = 256
VMEM = pl.BlockSpec(memory_space=pltpu.VMEM)
ANY = pl.BlockSpec(memory_space=pl.ANY)
SMALL = pltpu.CompilerParams(vmem_limit_bytes=32 * 2**20)
WHOLE = pltpu.CompilerParams(vmem_limit_bytes=215 * 2**18)
F32, BF16 = jnp.float32, jnp.bfloat16


class Plan:
    def __init__(self, detectors, samples, taps):
        self.detectors, self.samples, self.taps = detectors, samples, taps
        self.groups = (taps - 1) // BLOCK
        self.steps = samples // BLOCK
        self.lead = self.groups - 1
        self.blocks = samples // L
        self.reach = (taps - 1) // 2 // L
        self.out = self.blocks + 2 * self.reach


def filter_kernel(
    weights_in, tod, taps_in, owner_in, row_in, counts_in,
    out, weights, taps, owner, tile_row, counts, held, table, line, diagonal, sems, *, plan
):
    nd, steps, lead, groups = plan.detectors, plan.steps, plan.lead, plan.groups
    small = [
        pltpu.make_async_copy(src, dst, sems.at[steps + i])
        for i, (src, dst) in enumerate(
            ((taps_in.at[0], taps), (weights_in, weights), (owner_in, owner), (row_in, tile_row), (counts_in, counts))
        )
    ]
    big = [
        pltpu.make_async_copy(
            tod.at[0, :, b * BLOCK : (b + 1) * BLOCK], held.at[(lead + b) * nd : (lead + b + 1) * nd, :], sems.at[b]
        )
        for b in range(steps)
    ]
    for copy in small + big:
        copy.start()
    held[0 : lead * nd, :] = jnp.zeros((lead * nd, BLOCK), BF16)
    held[(lead + steps) * nd :, :] = jnp.zeros((lead * nd, BLOCK), BF16)
    line[...] = jnp.zeros_like(line)
    row = lax.broadcasted_iota(jnp.int32, (nd, L), 0)
    lane = lax.broadcasted_iota(jnp.int32, (nd, L), 1)
    for copy in small:
        copy.wait()
    spread = jnp.broadcast_to(jnp.pad(weights[...], ((0, 0), (0, L - nd))), (nd, L))
    column = jnp.sum(jnp.where(row == lane, spread, 0.0), axis=1, keepdims=True)
    for pair in range(groups // 2):
        for half in range(2):
            parts = []
            for j in (2 * pair, 2 * pair + 1):
                start = j * BLOCK + half * L
                part = taps[:, start : start + L].astype(F32) * column
                parts.append(jnp.take_along_axis(part, L - 1 - lane, axis=1))
            turned = jnp.concatenate(parts, axis=0).T
            high, low = two_terms(turned)
            at = (1 - half) * L
            table[at : at + L, pair * L : (pair + 1) * L] = high
            table[BLOCK + at : BLOCK + at + L, pair * L : (pair + 1) * L] = low
    last = jnp.broadcast_to(taps[:, groups * BLOCK : groups * BLOCK + 1].astype(F32) * column, (nd, L))
    row8 = lax.broadcasted_iota(jnp.int32, (8, L), 0)
    lane8 = lax.broadcasted_iota(jnp.int32, (8, L), 1)
    for copy in big:
        copy.wait()

    slots = diagonal.shape[0]
    count = steps + lead

    def product(v):
        half = groups // 2
        low = half if v + half <= lead else 0
        high = half if v + half >= lead + steps else groups
        x = held[(v + low) * nd : (v + high) * nd, :]
        both = jnp.dot(table[:, low * nd : high * nd], x, preferred_element_type=F32)
        diagonal[v % slots] = both[:BLOCK] + both[BLOCK:]

    def add_diagonals(tiles, at):
        total = direct = None
        for b in range(0, L, 8):
            part = tiles[0][b : b + 8]
            for other in tiles[1:]:
                part += other[b : b + 8]
            part = pltpu.roll(part, b + 1, 1, stride=1, stride_axis=0)
            kept = jnp.where(lane8 > row8 + b, part, 0.0)
            total = part if total is None else total + part
            direct = kept if direct is None else direct + kept
        line[at] += direct
        line[at + 1] += total - direct

    def corner(v, down, across):
        return diagonal[v % slots, down * L : (down + 1) * L, across * L : (across + 1) * L]

    product(0)
    for v in range(count):
        if v + 1 < count:
            product(v + 1)
        first = [corner(v, 0, 0)] + ([corner(v - 1, 1, 1)] if v else [])
        add_diagonals(first, 2 * v)
        add_diagonals([corner(v, 1, 0), corner(v, 0, 1)], 2 * v + 1)
        if v >= lead:
            for half in range(2):
                x = held[v * nd : (v + 1) * nd, half * L : (half + 1) * L]
                line[2 * (v - lead) + half] += (x.astype(F32) * last).reshape(nd // 8, 8, L).sum(0)
    add_diagonals([corner(count - 1, 1, 1)], 2 * count)
    out[0 : plan.out, :] = jnp.sum(line[0 : plan.out], axis=1)

    nb = plan.blocks
    pad = ((0, 0), (0, L - nb))
    target = jnp.pad(owner[...], pad) * TROWS + jnp.pad(tile_row[...], pad)
    kept = lax.broadcasted_iota(jnp.int32, (1, L), 1) < counts[0, 0]
    target = jnp.where(kept, target, -1)
    out[plan.out : plan.out + 8, :] = jnp.broadcast_to(target.astype(F32), (8, L))


def two_terms(x):
    high = x.astype(BF16)
    return high, (x - high.astype(F32)).astype(BF16)


def rows_of(target, first, count):
    row = lax.broadcasted_iota(jnp.int32, (count, target.shape[1]), 0).astype(F32) + first
    row = jnp.where(row < 0, -2.0, row)
    return (jnp.broadcast_to(target, row.shape) == row).astype(BF16)


def add_rows(picks, blocks):
    high, low = two_terms(blocks)
    both = jnp.dot(picks, jnp.concatenate([high, low], axis=1), preferred_element_type=F32)
    return both[:, :L] + both[:, L:]


def tile_rows_kernel(*refs, plan, reach):
    parts, (home, away, own, sem) = list(refs[:-4]), refs[-4:]
    copy = pltpu.make_async_copy(parts[0], own, sem)
    copy.start()
    nb, halo = plan.blocks, plan.reach
    me = lax.axis_index("tm")
    ext = TROWS + 2 * reach
    marks_at = ext + 2 * halo * len(parts)
    away[marks_at:, :] = jnp.full((away.shape[0] - marks_at, L), -1.0, F32)

    def add(some, first):
        for k, ref in some:
            at = ext + 2 * halo * k
            away[at : at + halo, :] = ref[0:halo, :]
            away[at + halo : at + 2 * halo, :] = ref[halo + nb : plan.out, :]
            away[marks_at + k : marks_at + k + 1, :] = ref[plan.out : plan.out + 1, :]
        target = jnp.concatenate([ref[plan.out : plan.out + 1, 0:nb] for _, ref in some], axis=1)
        blocks = jnp.concatenate([ref[halo : halo + nb, :] for _, ref in some], axis=0)
        for out, tile in ((home, me), (away, jnp.bitwise_xor(me, 1))):
            rows = add_rows(rows_of(target, (tile * TROWS - reach).astype(F32), ext), blocks)
            out[0:ext, :] = rows if first else out[0:ext, :] + rows

    if len(parts) > 1:
        add(list(enumerate(parts))[1:], True)
    copy.wait()
    add([(0, own)], len(parts) == 1)


def windows_kernel(*refs, plan, order, bands, reach):
    home, here, other, beam_rows, beam_cols, mixing, out, marks, tile = refs
    me = lax.axis_index("tm")
    mine = lax.axis_index("band") // 2
    nb, halo = plan.blocks, plan.reach
    ext = TROWS + 2 * reach
    after_rows = ext + 2 * halo * len(order)
    marks[...] = jnp.full_like(marks, -1.0)
    numbers = []
    for side, ref in enumerate((here, other)):
        for k, z in enumerate(order):
            t = jnp.bitwise_xor(me, 2 * z + side)
            marks[pl.ds(8 + t, 1), :] = ref[after_rows + k : after_rows + k + 1, :]
            numbers.append(t)
    targets = []
    for t in numbers:
        before = marks[pl.ds(7 + t, 1), :]
        after = marks[pl.ds(9 + t, 1), :]
        targets += [before[:, nb - halo : nb], after[:, 0:halo]]
    blocks = [here[ext:after_rows, :], other[ext:after_rows, :]]
    picks = rows_of(jnp.concatenate(targets, axis=1), (me * TROWS - reach).astype(F32), ext)
    tile[...] = home[...] + other[0:ext, :] + add_rows(picks, jnp.concatenate(blocks, axis=0))
    share = TROWS // bands
    wide = 2 * share + 2 * reach
    terms, taps = beam_rows.shape[1:]
    comps = mixing.shape[0]
    out[...] = jnp.zeros_like(out)
    pad = jnp.zeros((8, L - taps), F32)
    lane = lax.broadcasted_iota(jnp.int32, (8, L), 1)
    turn = jnp.where(lane < taps, taps - 1 - lane, lane)
    for h in range(bands // 2):
        start = pl.multiple_of(jnp.bitwise_xor(mine, h) * (2 * share), 8)
        out[h, 0:wide, :] = tile[pl.ds(start, wide), :]
        for k in range(terms):
            out[h, wide + k : wide + k + 1, 0:taps] = beam_rows[0, k : k + 1, :]
            profile = jnp.broadcast_to(beam_cols[0, k : k + 1, :], (8, taps))
            turned = jnp.take_along_axis(jnp.concatenate([profile, pad], axis=1), turn, axis=1)
            out[h, wide + terms + k : wide + terms + k + 1, :] = turned[0:1]
            for c in range(comps):
                at = wide + 2 * terms + c * terms + k
                out[h, at : at + 1, :] = jnp.broadcast_to(mixing[c, 0:1, k : k + 1], (1, L))


def dot3(a, b, dims):
    a0, a1 = two_terms(a)
    b0, b1 = two_terms(b)
    ka, kb = dims
    left = jnp.concatenate([a0, a0, a1], axis=ka)
    right = jnp.concatenate([b0, b1, b0], axis=kb)
    return lax.dot_general(left, right, (((ka,), (kb,)), ((), ())), preferred_element_type=F32)


def beam_kernel(*refs, share, reach, terms, comps, taps):
    ins, out = refs[:-1], refs[-1]
    core = lax.rem(lax.axis_index("band"), 2)
    wide = 2 * share + 2 * reach
    need = share + 2 * reach
    x = lax.broadcasted_iota(jnp.int32, (L, L), 0)
    c_in = lax.broadcasted_iota(jnp.int32, (L, L), 1)
    near = jnp.abs(c_in - x) <= reach
    totals = [None] * comps
    for ref in ins:
        for h in range(ref.shape[0]):
            rows = ref[h, pl.ds(pl.multiple_of(core * share, 8), need), :]
            mats = []
            for k in range(terms):
                spread = jnp.broadcast_to(ref[h, wide + k : wide + k + 1, :], (share, L))
                mats.append(pltpu.roll(spread, 0, 1, stride=1, stride_axis=0)[:, :need])
            rowed = dot3(jnp.concatenate(mats, axis=0), rows, (1, 0))
            for k in range(terms):
                at = wide + terms + k
                spread = jnp.broadcast_to(ref[h, at : at + 1, :], (L, L))
                cols = pltpu.roll(spread, L - reach, 1, stride=1, stride_axis=0)
                cols = jnp.where(near, cols, 0.0)
                beamed = dot3(rowed[k * share : (k + 1) * share], cols, (1, 0))
                for c in range(comps):
                    at = wide + 2 * terms + c * terms + k
                    part = beamed * ref[h, at : at + 1, :]
                    totals[c] = part if totals[c] is None else totals[c] + part
    for c in range(comps):
        out[c, 0] = totals[c]


def flip(x, axis, bits):
    count = lax.axis_size(axis)
    return lax.ppermute(x, axis, [(i, i ^ bits) for i in range(count)])


def on_device(
    tod, filter_taps, det_weights, owner, tile_row, block_counts, beam_rows, beam_cols, mixing
):
    detectors, samples = tod.shape[1:]
    taps = filter_taps.shape[2]
    plan = Plan(detectors, samples, taps)
    tms, bands = lax.axis_size("tm"), lax.axis_size("band")
    inner = 2
    outer = tms // inner
    terms, beam = beam_rows.shape[1:]
    reach = (beam - 1) // 2
    comps = mixing.shape[0]
    values = pl.pallas_call(
        functools.partial(filter_kernel, plan=plan),
        out_shape=jax.ShapeDtypeStruct((plan.out + 8, L), F32),
        in_specs=[ANY] * 6,
        out_specs=VMEM,
        scratch_shapes=[
            pltpu.VMEM((1, detectors), F32),
            pltpu.VMEM((detectors, taps), BF16),
            pltpu.VMEM((1, plan.blocks), jnp.int32),
            pltpu.VMEM((1, plan.blocks), jnp.int32),
            pltpu.SMEM((1, 1), jnp.int32),
            pltpu.VMEM(((plan.steps + 2 * plan.lead) * detectors, BLOCK), BF16),
            pltpu.VMEM((2 * BLOCK, plan.groups * detectors), BF16),
            pltpu.VMEM((plan.out + 8, 8, L), F32),
            pltpu.VMEM((3, BLOCK, BLOCK), F32),
            pltpu.SemaphoreType.DMA((plan.steps + 5,)),
        ],
        compiler_params=WHOLE,
        name="filter_blocks",
    )(det_weights, tod, filter_taps, owner[:, :, 0], tile_row, block_counts)
    order = list(range(outer))
    parts = [flip(values, "tm", k * inner) if k else values for k in order]
    ext = TROWS + 2 * reach
    sent = ext + 2 * plan.reach * outer + -(-outer // 8) * 8
    home, away = pl.pallas_call(
        functools.partial(tile_rows_kernel, plan=plan, reach=reach),
        out_shape=(jax.ShapeDtypeStruct((ext, L), F32), jax.ShapeDtypeStruct((sent, L), F32)),
        in_specs=[ANY] + [VMEM] * (outer - 1),
        scratch_shapes=[pltpu.VMEM((plan.out + 8, L), F32), pltpu.SemaphoreType.DMA],
        out_specs=(VMEM, VMEM),
        compiler_params=SMALL,
        name="tile_rows",
    )(*parts)
    other = flip(away, "tm", 1)
    share = TROWS // bands
    wide = 2 * share + 2 * reach
    extra = -(-(2 * terms + comps * terms) // 8) * 8
    windows = pl.pallas_call(
        functools.partial(windows_kernel, plan=plan, order=order, bands=bands, reach=reach),
        out_shape=jax.ShapeDtypeStruct((bands // 2, wide + extra, L), F32),
        in_specs=[VMEM] * 6,
        out_specs=VMEM,
        scratch_shapes=[pltpu.VMEM((16 + tms, L), F32), pltpu.VMEM((ext, L), F32)],
        compiler_params=SMALL,
        name="band_windows",
    )(home, away, other, beam_rows, beam_cols, mixing)
    own = windows[0:1]
    across = [flip(windows[h : h + 1], "band", 2 * h) for h in range(1, bands // 2)]
    mine = [own] + across
    other = [flip(m, "band", 1) for m in mine]
    return pl.pallas_call(
        functools.partial(beam_kernel, share=share, reach=reach, terms=terms, comps=comps, taps=beam),
        out_shape=jax.ShapeDtypeStruct((comps, 1, share, L), F32),
        in_specs=[VMEM] * (2 * len(mine)),
        out_specs=VMEM,
        compiler_params=SMALL,
        name="smooth_and_mix",
    )(*mine, *other)


def solution(mesh):
    placed = (
        P("band", None, "tm"),
        P("band", None, None),
        P("band", None),
        P("band", "tm", None),
        P("band", "tm"),
        P("band", "tm"),
        P("band", None, None),
        P("band", None, None),
        P(None, "band", None),
    )
    return jax.shard_map(
        on_device,
        mesh=mesh,
        in_specs=placed,
        out_specs=P(None, "tm", "band", None),
        check_vma=False,
    )
```

```python
import functools

import jax
import jax.numpy as jnp
from jax import lax
from jax.experimental import pallas as pl
from jax.experimental.pallas import tpu as pltpu
from jax.sharding import PartitionSpec as P

L = 128
TROWS = 128
BLOCK = 256
VMEM = pl.BlockSpec(memory_space=pltpu.VMEM)
ANY = pl.BlockSpec(memory_space=pl.ANY)
SMALL = pltpu.CompilerParams(vmem_limit_bytes=32 * 2**20)
WHOLE = pltpu.CompilerParams(vmem_limit_bytes=215 * 2**18)
F32, BF16 = jnp.float32, jnp.bfloat16


class Plan:
    def __init__(self, detectors, samples, taps):
        self.detectors, self.samples, self.taps = detectors, samples, taps
        self.groups = (taps - 1) // BLOCK
        self.steps = samples // BLOCK
        self.lead = self.groups - 1
        self.blocks = samples // L
        self.reach = (taps - 1) // 2 // L
        self.out = self.blocks + 2 * self.reach


def filter_kernel(
    weights_in, tod, taps_in, owner_in, row_in, counts_in,
    out, weights, taps, owner, tile_row, counts, held, table, line, diagonal, sems, *, plan
):
    nd, steps, lead, groups = plan.detectors, plan.steps, plan.lead, plan.groups
    small = [
        pltpu.make_async_copy(src, dst, sems.at[steps + i])
        for i, (src, dst) in enumerate(
            ((taps_in.at[0], taps), (weights_in, weights), (owner_in, owner), (row_in, tile_row), (counts_in, counts))
        )
    ]
    big = [
        pltpu.make_async_copy(
            tod.at[0, :, b * BLOCK : (b + 1) * BLOCK], held.at[(lead + b) * nd : (lead + b + 1) * nd, :], sems.at[b]
        )
        for b in range(steps)
    ]
    for copy in small + big:
        copy.start()
    held[0 : lead * nd, :] = jnp.zeros((lead * nd, BLOCK), BF16)
    held[(lead + steps) * nd :, :] = jnp.zeros((lead * nd, BLOCK), BF16)
    line[...] = jnp.zeros_like(line)
    row = lax.broadcasted_iota(jnp.int32, (nd, L), 0)
    lane = lax.broadcasted_iota(jnp.int32, (nd, L), 1)
    for copy in small:
        copy.wait()
    spread = jnp.broadcast_to(jnp.pad(weights[...], ((0, 0), (0, L - nd))), (nd, L))
    column = jnp.sum(jnp.where(row == lane, spread, 0.0), axis=1, keepdims=True)
    for pair in range(groups // 2):
        for half in range(2):
            parts = []
            for j in (2 * pair, 2 * pair + 1):
                start = j * BLOCK + half * L
                part = taps[:, start : start + L].astype(F32) * column
                parts.append(jnp.take_along_axis(part, L - 1 - lane, axis=1))
            turned = jnp.concatenate(parts, axis=0).T
            high, low = two_terms(turned)
            at = (1 - half) * L
            table[at : at + L, pair * L : (pair + 1) * L] = high
            table[BLOCK + at : BLOCK + at + L, pair * L : (pair + 1) * L] = low
    last = jnp.broadcast_to(taps[:, groups * BLOCK : groups * BLOCK + 1].astype(F32) * column, (nd, L))
    row8 = lax.broadcasted_iota(jnp.int32, (8, L), 0)
    lane8 = lax.broadcasted_iota(jnp.int32, (8, L), 1)
    for copy in big:
        copy.wait()

    slots = diagonal.shape[0]
    count = steps + lead

    def product(v):
        half = groups // 2
        low = half if v + half <= lead else 0
        high = half if v + half >= lead + steps else groups
        x = held[(v + low) * nd : (v + high) * nd, :]
        both = jnp.dot(table[:, low * nd : high * nd], x, preferred_element_type=F32)
        diagonal[v % slots] = both[:BLOCK] + both[BLOCK:]

    def add_diagonals(tiles, at):
        total = direct = None
        for b in range(0, L, 8):
            part = tiles[0][b : b + 8]
            for other in tiles[1:]:
                part += other[b : b + 8]
            part = pltpu.roll(part, b + 1, 1, stride=1, stride_axis=0)
            kept = jnp.where(lane8 > row8 + b, part, 0.0)
            total = part if total is None else total + part
            direct = kept if direct is None else direct + kept
        line[at] += direct
        line[at + 1] += total - direct

    def corner(v, down, across):
        return diagonal[v % slots, down * L : (down + 1) * L, across * L : (across + 1) * L]

    product(0)
    for v in range(count):
        if v + 1 < count:
            product(v + 1)
        first = [corner(v, 0, 0)] + ([corner(v - 1, 1, 1)] if v else [])
        add_diagonals(first, 2 * v)
        add_diagonals([corner(v, 1, 0), corner(v, 0, 1)], 2 * v + 1)
        if v >= lead:
            for half in range(2):
                x = held[v * nd : (v + 1) * nd, half * L : (half + 1) * L]
                line[2 * (v - lead) + half] += (x.astype(F32) * last).reshape(nd // 8, 8, L).sum(0)
    add_diagonals([corner(count - 1, 1, 1)], 2 * count)
    out[0 : plan.out, :] = jnp.sum(line[0 : plan.out], axis=1)

    nb = plan.blocks
    pad = ((0, 0), (0, L - nb))
    target = jnp.pad(owner[...], pad) * TROWS + jnp.pad(tile_row[...], pad)
    kept = lax.broadcasted_iota(jnp.int32, (1, L), 1) < counts[0, 0]
    target = jnp.where(kept, target, -1)
    out[plan.out : plan.out + 8, :] = jnp.broadcast_to(target.astype(F32), (8, L))


def two_terms(x):
    high = x.astype(BF16)
    return high, (x - high.astype(F32)).astype(BF16)


def rows_of(target, first, count):
    row = lax.broadcasted_iota(jnp.int32, (count, target.shape[1]), 0).astype(F32) + first
    row = jnp.where(row < 0, -2.0, row)
    return (jnp.broadcast_to(target, row.shape) == row).astype(BF16)


def add_rows(picks, blocks):
    high, low = two_terms(blocks)
    both = jnp.dot(picks, jnp.concatenate([high, low], axis=1), preferred_element_type=F32)
    return both[:, :L] + both[:, L:]


def gather_rounds(count):
    if count != 4:
        return [[(i, i ^ k) for i in range(count)] for k in range(1, count)]
    last = count - 1
    ring = [[(i, (i + k) % last) for i in range(last)] for k in range(1, last)]
    return ring + [[(i, last), (last, i)] for i in range(last)]


def slots(rounds, count):
    found = []
    seen = [0] * count
    for r, pairs in enumerate(rounds):
        for _, target in pairs:
            if seen[target] == len(found):
                found.append({})
            found[seen[target]].setdefault(r, []).append(target)
            seen[target] += 1
    return [sorted(slot.items()) for slot in found]


def sources(rounds, count):
    table = [[] for _ in range(count)]
    for pairs in rounds:
        for source, target in pairs:
            table[target].append(source)
    return [[table[p][k] for p in range(count)] for k in range(count - 1)]


def pick(place, values):
    result = jnp.int32(values[0])
    for p, value in enumerate(values):
        result = jnp.where(place == p, value, result)
    return result


def tile_rows_kernel(*refs, plan, reach, rounds, outer):
    arrived, (home, away, kept) = refs[:-3], refs[-3:]
    nb, halo = plan.blocks, plan.reach
    me = lax.axis_index("tm")
    parts = [arrived[0]]
    if rounds:
        place = me // 2
        for k, slot in enumerate(slots(rounds, outer)):
            total = None
            for r, places in slot:
                part = arrived[1 + r][...]
                if len(places) < outer:
                    hit = functools.reduce(jnp.logical_or, [place == p for p in places])
                    part = jnp.where(hit, part, 0.0)
                total = part if total is None else total + part
            kept[k] = total
            parts.append(kept.at[k])
    ext = TROWS + 2 * reach
    marks_at = ext + 2 * halo * len(parts)
    away[marks_at:, :] = jnp.full((away.shape[0] - marks_at, L), -1.0, F32)

    for k, ref in enumerate(parts):
        at = ext + 2 * halo * k
        away[at : at + halo, :] = ref[0:halo, :]
        away[at + halo : at + 2 * halo, :] = ref[halo + nb : plan.out, :]
        away[marks_at + k : marks_at + k + 1, :] = ref[plan.out : plan.out + 1, :]
    target = jnp.concatenate([ref[plan.out : plan.out + 1, 0:nb] for ref in parts], axis=1)
    blocks = jnp.concatenate([ref[halo : halo + nb, :] for ref in parts], axis=0)
    for out, tile in ((home, me), (away, jnp.bitwise_xor(me, 1))):
        out[0:ext, :] = add_rows(rows_of(target, (tile * TROWS - reach).astype(F32), ext), blocks)


def windows_kernel(*refs, plan, origins, outer, bands, reach):
    home, here, other, beam_rows, beam_cols, mixing, out, marks, tile = refs
    me = lax.axis_index("tm")
    mine = lax.axis_index("band") // 2
    nb, halo = plan.blocks, plan.reach
    ext = TROWS + 2 * reach
    after_rows = ext + 2 * halo * outer
    marks[...] = jnp.full_like(marks, -1.0)
    numbers = []
    for side, ref in enumerate((here, other)):
        for k in range(outer):
            place = pick(me // 2, origins[k - 1]) if k else me // 2
            t = 2 * place + jnp.bitwise_xor(lax.rem(me, 2), side)
            marks[pl.ds(8 + t, 1), :] = ref[after_rows + k : after_rows + k + 1, :]
            numbers.append(t)
    targets = []
    for t in numbers:
        before = marks[pl.ds(7 + t, 1), :]
        after = marks[pl.ds(9 + t, 1), :]
        targets += [before[:, nb - halo : nb], after[:, 0:halo]]
    blocks = [here[ext:after_rows, :], other[ext:after_rows, :]]
    picks = rows_of(jnp.concatenate(targets, axis=1), (me * TROWS - reach).astype(F32), ext)
    tile[...] = home[...] + other[0:ext, :] + add_rows(picks, jnp.concatenate(blocks, axis=0))
    share = TROWS // bands
    wide = 2 * share + 2 * reach
    terms, taps = beam_rows.shape[1:]
    comps = mixing.shape[0]
    out[...] = jnp.zeros_like(out)
    pad = jnp.zeros((8, L - taps), F32)
    lane = lax.broadcasted_iota(jnp.int32, (8, L), 1)
    turn = jnp.where(lane < taps, taps - 1 - lane, lane)
    for h in range(bands // 2):
        start = pl.multiple_of(jnp.bitwise_xor(mine, h) * (2 * share), 8)
        out[h, 0:wide, :] = tile[pl.ds(start, wide), :]
        for k in range(terms):
            out[h, wide + k : wide + k + 1, 0:taps] = beam_rows[0, k : k + 1, :]
            profile = jnp.broadcast_to(beam_cols[0, k : k + 1, :], (8, taps))
            turned = jnp.take_along_axis(jnp.concatenate([profile, pad], axis=1), turn, axis=1)
            out[h, wide + terms + k : wide + terms + k + 1, :] = turned[0:1]
            for c in range(comps):
                at = wide + 2 * terms + c * terms + k
                out[h, at : at + 1, :] = jnp.broadcast_to(mixing[c, 0:1, k : k + 1], (1, L))


def dot3(a, b, dims):
    a0, a1 = two_terms(a)
    b0, b1 = two_terms(b)
    ka, kb = dims
    left = jnp.concatenate([a0, a0, a1], axis=ka)
    right = jnp.concatenate([b0, b1, b0], axis=kb)
    return lax.dot_general(left, right, (((ka,), (kb,)), ((), ())), preferred_element_type=F32)


def beam_kernel(*refs, share, reach, terms, comps, taps):
    ins, out = refs[:-1], refs[-1]
    core = lax.rem(lax.axis_index("band"), 2)
    wide = 2 * share + 2 * reach
    need = share + 2 * reach
    x = lax.broadcasted_iota(jnp.int32, (L, L), 0)
    c_in = lax.broadcasted_iota(jnp.int32, (L, L), 1)
    near = jnp.abs(c_in - x) <= reach
    totals = [None] * comps
    for ref in ins:
        for h in range(ref.shape[0]):
            rows = ref[h, pl.ds(pl.multiple_of(core * share, 8), need), :]
            mats = []
            for k in range(terms):
                spread = jnp.broadcast_to(ref[h, wide + k : wide + k + 1, :], (share, L))
                mats.append(pltpu.roll(spread, 0, 1, stride=1, stride_axis=0)[:, :need])
            rowed = dot3(jnp.concatenate(mats, axis=0), rows, (1, 0))
            for k in range(terms):
                at = wide + terms + k
                spread = jnp.broadcast_to(ref[h, at : at + 1, :], (L, L))
                cols = pltpu.roll(spread, L - reach, 1, stride=1, stride_axis=0)
                cols = jnp.where(near, cols, 0.0)
                beamed = dot3(rowed[k * share : (k + 1) * share], cols, (1, 0))
                for c in range(comps):
                    at = wide + 2 * terms + c * terms + k
                    part = beamed * ref[h, at : at + 1, :]
                    totals[c] = part if totals[c] is None else totals[c] + part
    for c in range(comps):
        out[c, 0] = totals[c]


def flip(x, axis, bits):
    count = lax.axis_size(axis)
    return lax.ppermute(x, axis, [(i, i ^ bits) for i in range(count)])


def on_device(
    tod, filter_taps, det_weights, owner, tile_row, block_counts, beam_rows, beam_cols, mixing
):
    detectors, samples = tod.shape[1:]
    taps = filter_taps.shape[2]
    plan = Plan(detectors, samples, taps)
    tms, bands = lax.axis_size("tm"), lax.axis_size("band")
    inner = 2
    outer = tms // inner
    terms, beam = beam_rows.shape[1:]
    reach = (beam - 1) // 2
    comps = mixing.shape[0]
    values = pl.pallas_call(
        functools.partial(filter_kernel, plan=plan),
        out_shape=jax.ShapeDtypeStruct((plan.out + 8, L), F32),
        in_specs=[ANY] * 6,
        out_specs=VMEM,
        scratch_shapes=[
            pltpu.VMEM((1, detectors), F32),
            pltpu.VMEM((detectors, taps), BF16),
            pltpu.VMEM((1, plan.blocks), jnp.int32),
            pltpu.VMEM((1, plan.blocks), jnp.int32),
            pltpu.SMEM((1, 1), jnp.int32),
            pltpu.VMEM(((plan.steps + 2 * plan.lead) * detectors, BLOCK), BF16),
            pltpu.VMEM((2 * BLOCK, plan.groups * detectors), BF16),
            pltpu.VMEM((plan.out + 8, 8, L), F32),
            pltpu.VMEM((3, BLOCK, BLOCK), F32),
            pltpu.SemaphoreType.DMA((plan.steps + 5,)),
        ],
        compiler_params=WHOLE,
        name="filter_blocks",
    )(det_weights, tod, filter_taps, owner[:, :, 0], tile_row, block_counts)
    rounds = gather_rounds(outer)
    pairs = [[(s * inner + i, t * inner + i) for s, t in r for i in range(inner)] for r in rounds]
    parts = [values] + [lax.ppermute(values, "tm", p) for p in pairs]
    ext = TROWS + 2 * reach
    sent = ext + 2 * plan.reach * outer + -(-outer // 8) * 8
    home, away = pl.pallas_call(
        functools.partial(tile_rows_kernel, plan=plan, reach=reach, rounds=rounds, outer=outer),
        out_shape=(jax.ShapeDtypeStruct((ext, L), F32), jax.ShapeDtypeStruct((sent, L), F32)),
        in_specs=[VMEM] * len(parts),
        scratch_shapes=[pltpu.VMEM((max(outer - 1, 1), plan.out + 8, L), F32)],
        out_specs=(VMEM, VMEM),
        compiler_params=SMALL,
        name="tile_rows",
    )(*parts)
    other = flip(away, "tm", 1)
    share = TROWS // bands
    wide = 2 * share + 2 * reach
    extra = -(-(2 * terms + comps * terms) // 8) * 8
    windows = pl.pallas_call(
        functools.partial(windows_kernel, plan=plan, origins=sources(rounds, outer), outer=outer, bands=bands, reach=reach),
        out_shape=jax.ShapeDtypeStruct((bands // 2, wide + extra, L), F32),
        in_specs=[VMEM] * 6,
        out_specs=VMEM,
        scratch_shapes=[pltpu.VMEM((16 + tms, L), F32), pltpu.VMEM((ext, L), F32)],
        compiler_params=SMALL,
        name="band_windows",
    )(home, away, other, beam_rows, beam_cols, mixing)
    own = windows[0:1]
    across = [flip(windows[h : h + 1], "band", 2 * h) for h in range(1, bands // 2)]
    mine = [own] + across
    other = [flip(m, "band", 1) for m in mine]
    return pl.pallas_call(
        functools.partial(beam_kernel, share=share, reach=reach, terms=terms, comps=comps, taps=beam),
        out_shape=jax.ShapeDtypeStruct((comps, 1, share, L), F32),
        in_specs=[VMEM] * (2 * len(mine)),
        out_specs=VMEM,
        compiler_params=SMALL,
        name="smooth_and_mix",
    )(*mine, *other)


def solution(mesh):
    placed = (
        P("band", None, "tm"),
        P("band", None, None),
        P("band", None),
        P("band", "tm", None),
        P("band", "tm"),
        P("band", "tm"),
        P("band", None, None),
        P("band", None, None),
        P(None, "band", None),
    )
    return jax.shard_map(
        on_device,
        mesh=mesh,
        in_specs=placed,
        out_specs=P(None, "tm", "band", None),
        check_vma=False,
    )
```

```python
import functools

import jax
import jax.numpy as jnp
from jax import lax
from jax.experimental import pallas as pl
from jax.experimental.pallas import tpu as pltpu
from jax.sharding import PartitionSpec as P

L = 128
TROWS = 128
BLOCK = 256
VMEM = pl.BlockSpec(memory_space=pltpu.VMEM)
ANY = pl.BlockSpec(memory_space=pl.ANY)
SMALL = pltpu.CompilerParams(vmem_limit_bytes=32 * 2**20)
WHOLE = pltpu.CompilerParams(vmem_limit_bytes=48 * 2**20)
F32, BF16 = jnp.float32, jnp.bfloat16


class Plan:
    def __init__(self, detectors, samples, taps):
        self.detectors, self.samples, self.taps = detectors, samples, taps
        self.groups = (taps - 1) // BLOCK
        self.steps = samples // BLOCK
        self.lead = self.groups - 1
        self.blocks = samples // L
        self.reach = (taps - 1) // 2 // L
        self.out = self.blocks + 2 * self.reach


def filter_kernel(
    weights_in, tod, taps_in, owner_in, row_in, counts_in,
    out, weights, taps, owner, tile_row, counts, held, table, line, diagonal, sems, *, plan
):
    nd, steps, lead, groups = plan.detectors, plan.steps, plan.lead, plan.groups
    small = [
        pltpu.make_async_copy(src, dst, sems.at[steps + i])
        for i, (src, dst) in enumerate(
            ((taps_in.at[0], taps), (weights_in, weights), (owner_in, owner), (row_in, tile_row), (counts_in, counts))
        )
    ]
    big = [
        pltpu.make_async_copy(
            tod.at[0, :, b * BLOCK : (b + 1) * BLOCK], held.at[(lead + b) * nd : (lead + b + 1) * nd, :], sems.at[b]
        )
        for b in range(steps)
    ]
    for copy in small + big:
        copy.start()
    held[0 : lead * nd, :] = jnp.zeros((lead * nd, BLOCK), BF16)
    held[(lead + steps) * nd :, :] = jnp.zeros((lead * nd, BLOCK), BF16)
    line[...] = jnp.zeros_like(line)
    row = lax.broadcasted_iota(jnp.int32, (nd, L), 0)
    lane = lax.broadcasted_iota(jnp.int32, (nd, L), 1)
    for copy in small:
        copy.wait()
    spread = jnp.broadcast_to(jnp.pad(weights[...], ((0, 0), (0, L - nd))), (nd, L))
    column = jnp.sum(jnp.where(row == lane, spread, 0.0), axis=1, keepdims=True)
    for pair in range(groups // 2):
        for half in range(2):
            parts = []
            for j in (2 * pair, 2 * pair + 1):
                start = j * BLOCK + half * L
                part = taps[:, start : start + L].astype(F32) * column
                parts.append(jnp.take_along_axis(part, L - 1 - lane, axis=1))
            turned = jnp.concatenate(parts, axis=0).T
            high, low = two_terms(turned)
            at = (1 - half) * L
            table[at : at + L, pair * L : (pair + 1) * L] = high
            table[BLOCK + at : BLOCK + at + L, pair * L : (pair + 1) * L] = low
    last = jnp.broadcast_to(taps[:, groups * BLOCK : groups * BLOCK + 1].astype(F32) * column, (nd, L))
    row8 = lax.broadcasted_iota(jnp.int32, (8, L), 0)
    lane8 = lax.broadcasted_iota(jnp.int32, (8, L), 1)
    for copy in big:
        copy.wait()

    slots = diagonal.shape[0]
    count = steps + lead

    def product(v):
        half = groups // 2
        low = half if v + half <= lead else 0
        high = half if v + half >= lead + steps else groups
        x = held[(v + low) * nd : (v + high) * nd, :]
        both = jnp.dot(table[:, low * nd : high * nd], x, preferred_element_type=F32)
        diagonal[v % slots] = both[:BLOCK] + both[BLOCK:]

    def add_diagonals(tiles, at):
        total = direct = None
        for b in range(0, L, 8):
            part = tiles[0][b : b + 8]
            for other in tiles[1:]:
                part += other[b : b + 8]
            part = pltpu.roll(part, b + 1, 1, stride=1, stride_axis=0)
            kept = jnp.where(lane8 > row8 + b, part, 0.0)
            total = part if total is None else total + part
            direct = kept if direct is None else direct + kept
        line[at] += direct
        line[at + 1] += total - direct

    def corner(v, down, across):
        return diagonal[v % slots, down * L : (down + 1) * L, across * L : (across + 1) * L]

    product(0)
    for v in range(count):
        if v + 1 < count:
            product(v + 1)
        first = [corner(v, 0, 0)] + ([corner(v - 1, 1, 1)] if v else [])
        add_diagonals(first, 2 * v)
        add_diagonals([corner(v, 1, 0), corner(v, 0, 1)], 2 * v + 1)
        if v >= lead:
            for half in range(2):
                x = held[v * nd : (v + 1) * nd, half * L : (half + 1) * L]
                line[2 * (v - lead) + half] += (x.astype(F32) * last).reshape(nd // 8, 8, L).sum(0)
    add_diagonals([corner(count - 1, 1, 1)], 2 * count)
    out[0 : plan.out, :] = jnp.sum(line[0 : plan.out], axis=1)

    nb = plan.blocks
    pad = ((0, 0), (0, L - nb))
    target = jnp.pad(owner[...], pad) * TROWS + jnp.pad(tile_row[...], pad)
    kept = lax.broadcasted_iota(jnp.int32, (1, L), 1) < counts[0, 0]
    target = jnp.where(kept, target, -1)
    out[plan.out : plan.out + 8, :] = jnp.broadcast_to(target.astype(F32), (8, L))


def two_terms(x):
    high = x.astype(BF16)
    return high, (x - high.astype(F32)).astype(BF16)


def rows_of(target, first, count):
    row = lax.broadcasted_iota(jnp.int32, (count, target.shape[1]), 0).astype(F32) + first
    row = jnp.where(row < 0, -2.0, row)
    return (jnp.broadcast_to(target, row.shape) == row).astype(BF16)


def add_rows(picks, blocks):
    high, low = two_terms(blocks)
    both = jnp.dot(picks, jnp.concatenate([high, low], axis=1), preferred_element_type=F32)
    return both[:, :L] + both[:, L:]


def tile_rows_kernel(*refs, plan, reach):
    parts, (home, away, own, sem) = list(refs[:-4]), refs[-4:]
    copy = pltpu.make_async_copy(parts[0], own, sem)
    copy.start()
    nb, halo = plan.blocks, plan.reach
    me = lax.axis_index("tm")
    ext = TROWS + 2 * reach
    marks_at = ext + 2 * halo * len(parts)
    away[marks_at:, :] = jnp.full((away.shape[0] - marks_at, L), -1.0, F32)

    def add(some, first):
        for k, ref in some:
            at = ext + 2 * halo * k
            away[at : at + halo, :] = ref[0:halo, :]
            away[at + halo : at + 2 * halo, :] = ref[halo + nb : plan.out, :]
            away[marks_at + k : marks_at + k + 1, :] = ref[plan.out : plan.out + 1, :]
        target = jnp.concatenate([ref[plan.out : plan.out + 1, 0:nb] for _, ref in some], axis=1)
        blocks = jnp.concatenate([ref[halo : halo + nb, :] for _, ref in some], axis=0)
        for out, tile in ((home, me), (away, jnp.bitwise_xor(me, 1))):
            rows = add_rows(rows_of(target, (tile * TROWS - reach).astype(F32), ext), blocks)
            out[0:ext, :] = rows if first else out[0:ext, :] + rows

    if len(parts) > 1:
        add(list(enumerate(parts))[1:], True)
    copy.wait()
    add([(0, own)], len(parts) == 1)


def windows_kernel(*refs, plan, order, bands, reach):
    home, here, other, beam_rows, beam_cols, mixing, out, marks, tile = refs
    me = lax.axis_index("tm")
    mine = lax.axis_index("band") // 2
    nb, halo = plan.blocks, plan.reach
    ext = TROWS + 2 * reach
    after_rows = ext + 2 * halo * len(order)
    marks[...] = jnp.full_like(marks, -1.0)
    numbers = []
    for side, ref in enumerate((here, other)):
        for k, z in enumerate(order):
            t = jnp.bitwise_xor(me, 2 * z + side)
            marks[pl.ds(8 + t, 1), :] = ref[after_rows + k : after_rows + k + 1, :]
            numbers.append(t)
    targets = []
    for t in numbers:
        before = marks[pl.ds(7 + t, 1), :]
        after = marks[pl.ds(9 + t, 1), :]
        targets += [before[:, nb - halo : nb], after[:, 0:halo]]
    blocks = [here[ext:after_rows, :], other[ext:after_rows, :]]
    picks = rows_of(jnp.concatenate(targets, axis=1), (me * TROWS - reach).astype(F32), ext)
    tile[...] = home[...] + other[0:ext, :] + add_rows(picks, jnp.concatenate(blocks, axis=0))
    share = TROWS // bands
    wide = 2 * share + 2 * reach
    terms, taps = beam_rows.shape[1:]
    comps = mixing.shape[0]
    out[...] = jnp.zeros_like(out)
    pad = jnp.zeros((8, L - taps), F32)
    lane = lax.broadcasted_iota(jnp.int32, (8, L), 1)
    turn = jnp.where(lane < taps, taps - 1 - lane, lane)
    for h in range(bands // 2):
        start = pl.multiple_of(jnp.bitwise_xor(mine, h) * (2 * share), 8)
        out[h, 0:wide, :] = tile[pl.ds(start, wide), :]
        for k in range(terms):
            out[h, wide + k : wide + k + 1, 0:taps] = beam_rows[0, k : k + 1, :]
            profile = jnp.broadcast_to(beam_cols[0, k : k + 1, :], (8, taps))
            turned = jnp.take_along_axis(jnp.concatenate([profile, pad], axis=1), turn, axis=1)
            out[h, wide + terms + k : wide + terms + k + 1, :] = turned[0:1]
            for c in range(comps):
                at = wide + 2 * terms + c * terms + k
                out[h, at : at + 1, :] = jnp.broadcast_to(mixing[c, 0:1, k : k + 1], (1, L))


def dot3(a, b, dims):
    a0, a1 = two_terms(a)
    b0, b1 = two_terms(b)
    ka, kb = dims
    left = jnp.concatenate([a0, a0, a1], axis=ka)
    right = jnp.concatenate([b0, b1, b0], axis=kb)
    return lax.dot_general(left, right, (((ka,), (kb,)), ((), ())), preferred_element_type=F32)


def beam_kernel(*refs, windows, share, reach, terms, comps):
    ins, sofar, out = refs[:windows], refs[windows:-1], refs[-1]
    core = lax.rem(lax.axis_index("band"), 2)
    wide = 2 * share + 2 * reach
    need = share + 2 * reach
    x = lax.broadcasted_iota(jnp.int32, (L, L), 0)
    c_in = lax.broadcasted_iota(jnp.int32, (L, L), 1)
    near = jnp.abs(c_in - x) <= reach
    totals = [sofar[0][c, 0] if sofar else None for c in range(comps)]
    for ref in ins:
        for h in range(ref.shape[0]):
            rows = ref[h, pl.ds(pl.multiple_of(core * share, 8), need), :]
            mats = []
            for k in range(terms):
                spread = jnp.broadcast_to(ref[h, wide + k : wide + k + 1, :], (share, L))
                mats.append(pltpu.roll(spread, 0, 1, stride=1, stride_axis=0)[:, :need])
            rowed = dot3(jnp.concatenate(mats, axis=0), rows, (1, 0))
            for k in range(terms):
                at = wide + terms + k
                spread = jnp.broadcast_to(ref[h, at : at + 1, :], (L, L))
                cols = pltpu.roll(spread, L - reach, 1, stride=1, stride_axis=0)
                cols = jnp.where(near, cols, 0.0)
                beamed = dot3(rowed[k * share : (k + 1) * share], cols, (1, 0))
                for c in range(comps):
                    at = wide + 2 * terms + c * terms + k
                    part = beamed * ref[h, at : at + 1, :]
                    totals[c] = part if totals[c] is None else totals[c] + part
    for c in range(comps):
        out[c, 0] = totals[c]


def flip(x, axis, bits):
    count = lax.axis_size(axis)
    return lax.ppermute(x, axis, [(i, i ^ bits) for i in range(count)])


def on_device(
    tod, filter_taps, det_weights, owner, tile_row, block_counts, beam_rows, beam_cols, mixing
):
    detectors, samples = tod.shape[1:]
    taps = filter_taps.shape[2]
    plan = Plan(detectors, samples, taps)
    tms, bands = lax.axis_size("tm"), lax.axis_size("band")
    inner = 2
    outer = tms // inner
    terms, beam = beam_rows.shape[1:]
    reach = (beam - 1) // 2
    comps = mixing.shape[0]
    inputs = (det_weights, tod, filter_taps, owner[:, :, 0], tile_row)
    values = pl.pallas_call(
        functools.partial(filter_kernel, plan=plan),
        out_shape=jax.ShapeDtypeStruct((plan.out + 8, L), F32),
        in_specs=[ANY] * 6,
        out_specs=VMEM,
        scratch_shapes=[
            pltpu.VMEM((1, detectors), F32),
            pltpu.VMEM((detectors, taps), BF16),
            pltpu.VMEM((1, plan.blocks), jnp.int32),
            pltpu.VMEM((1, plan.blocks), jnp.int32),
            pltpu.SMEM((1, 1), jnp.int32),
            pltpu.VMEM(((plan.steps + 2 * plan.lead) * detectors, BLOCK), BF16),
            pltpu.VMEM((2 * BLOCK, plan.groups * detectors), BF16),
            pltpu.VMEM((plan.out + 8, 8, L), F32),
            pltpu.VMEM((3, BLOCK, BLOCK), F32),
            pltpu.SemaphoreType.DMA((plan.steps + 5,)),
        ],
        compiler_params=WHOLE,
        name="filter_blocks",
    )(*[pltpu.with_memory_space_constraint(v, pltpu.HBM) for v in inputs], block_counts)
    order = list(range(outer))
    parts = [flip(values, "tm", k * inner) if k else values for k in order]
    ext = TROWS + 2 * reach
    sent = ext + 2 * plan.reach * outer + -(-outer // 8) * 8
    home, away = pl.pallas_call(
        functools.partial(tile_rows_kernel, plan=plan, reach=reach),
        out_shape=(jax.ShapeDtypeStruct((ext, L), F32), jax.ShapeDtypeStruct((sent, L), F32)),
        in_specs=[ANY] + [VMEM] * (outer - 1),
        scratch_shapes=[pltpu.VMEM((plan.out + 8, L), F32), pltpu.SemaphoreType.DMA],
        out_specs=(VMEM, VMEM),
        compiler_params=SMALL,
        name="tile_rows",
    )(*parts)
    other = flip(away, "tm", 1)
    share = TROWS // bands
    wide = 2 * share + 2 * reach
    extra = -(-(2 * terms + comps * terms) // 8) * 8
    windows = pl.pallas_call(
        functools.partial(windows_kernel, plan=plan, order=order, bands=bands, reach=reach),
        out_shape=jax.ShapeDtypeStruct((bands // 2, wide + extra, L), F32),
        in_specs=[VMEM] * 6,
        out_specs=VMEM,
        scratch_shapes=[pltpu.VMEM((16 + tms, L), F32), pltpu.VMEM((ext, L), F32)],
        compiler_params=SMALL,
        name="band_windows",
    )(home, away, other, beam_rows, beam_cols, mixing)
    own = windows[0:1]
    across = [flip(windows[h : h + 1], "band", 2 * h) for h in range(1, bands // 2)]
    smooth = functools.partial(beam_kernel, share=share, reach=reach, terms=terms, comps=comps)

    def add_beams(windows, *sofar):
        return pl.pallas_call(
            functools.partial(smooth, windows=len(windows)),
            out_shape=jax.ShapeDtypeStruct((comps, 1, share, L), F32),
            in_specs=[VMEM] * (len(windows) + len(sofar)),
            out_specs=VMEM,
            compiler_params=SMALL,
            cost_estimate=pl.CostEstimate(flops=10**9, bytes_accessed=10**6, transcendentals=0),
            name="smooth_and_mix",
        )(*windows, *sofar)

    result = add_beams([own])
    result = add_beams([flip(own, "band", 1)] + across, result)
    return add_beams([flip(window, "band", 1) for window in across], result)


def solution(mesh):
    placed = (
        P("band", None, "tm"),
        P("band", None, None),
        P("band", None),
        P("band", "tm", None),
        P("band", "tm"),
        P("band", "tm"),
        P("band", None, None),
        P("band", None, None),
        P(None, "band", None),
    )
    return jax.shard_map(
        on_device,
        mesh=mesh,
        in_specs=placed,
        out_specs=P(None, "tm", "band", None),
        check_vma=False,
    )
```

```python
import functools

import jax
import jax.numpy as jnp
from jax import lax
from jax.experimental import pallas as pl
from jax.experimental.pallas import tpu as pltpu
from jax.sharding import PartitionSpec as P

L = 128
TROWS = 128
BLOCK = 256
VMEM = pl.BlockSpec(memory_space=pltpu.VMEM)
ANY = pl.BlockSpec(memory_space=pl.ANY)
SMALL = pltpu.CompilerParams(vmem_limit_bytes=32 * 2**20)
WHOLE = pltpu.CompilerParams(vmem_limit_bytes=48 * 2**20)
F32, BF16, FP8 = jnp.float32, jnp.bfloat16, jnp.float8_e4m3fn
TOP = 256.0
TINY = 1e-30


class Plan:
    def __init__(self, detectors, samples, taps):
        self.detectors, self.samples, self.taps = detectors, samples, taps
        self.groups = (taps - 1) // BLOCK
        self.steps = samples // BLOCK
        self.lead = self.groups - 1
        self.blocks = samples // L
        self.reach = (taps - 1) // 2 // L
        self.out = self.blocks + 2 * self.reach


def filter_kernel(
    weights_in, tod, taps_in, owner_in, row_in, counts_in,
    out, weights, taps, owner, tile_row, counts, held, held8, table, rest, table8, line, diagonal, sems, *, plan
):
    nd, steps, lead, groups = plan.detectors, plan.steps, plan.lead, plan.groups
    small = [
        pltpu.make_async_copy(src, dst, sems.at[steps + i])
        for i, (src, dst) in enumerate(
            ((taps_in.at[0], taps), (weights_in, weights), (owner_in, owner), (row_in, tile_row), (counts_in, counts))
        )
    ]
    big = [
        pltpu.make_async_copy(
            tod.at[0, :, b * BLOCK : (b + 1) * BLOCK], held.at[(lead + b) * nd : (lead + b + 1) * nd, :], sems.at[b]
        )
        for b in range(steps)
    ]
    for copy in small + big:
        copy.start()
    held[0 : lead * nd, :] = jnp.zeros((lead * nd, BLOCK), BF16)
    held[(lead + steps) * nd :, :] = jnp.zeros((lead * nd, BLOCK), BF16)
    held8[0 : lead * nd, :] = jnp.zeros((lead * nd, BLOCK), FP8)
    held8[(lead + steps) * nd :, :] = jnp.zeros((lead * nd, BLOCK), FP8)
    line[...] = jnp.zeros_like(line)
    row = lax.broadcasted_iota(jnp.int32, (nd, L), 0)
    lane = lax.broadcasted_iota(jnp.int32, (nd, L), 1)
    for copy in small:
        copy.wait()
    spread = jnp.broadcast_to(jnp.pad(weights[...], ((0, 0), (0, L - nd))), (nd, L))
    column = jnp.sum(jnp.where(row == lane, spread, 0.0), axis=1, keepdims=True)
    for pair in range(groups // 2):
        for half in range(2):
            parts = []
            for j in (2 * pair, 2 * pair + 1):
                start = j * BLOCK + half * L
                part = taps[:, start : start + L].astype(F32) * column
                parts.append(jnp.take_along_axis(part, L - 1 - lane, axis=1))
            turned = jnp.concatenate(parts, axis=0).T
            high = turned.astype(BF16)
            at = (1 - half) * L
            table[at : at + L, pair * L : (pair + 1) * L] = high
            rest[at : at + L, pair * L : (pair + 1) * L] = turned - high.astype(F32)
    last = jnp.broadcast_to(taps[:, groups * BLOCK : groups * BLOCK + 1].astype(F32) * column, (nd, L))
    row8 = lax.broadcasted_iota(jnp.int32, (8, L), 0)
    lane8 = lax.broadcasted_iota(jnp.int32, (8, L), 1)
    for copy in big:
        copy.wait()

    loud = jnp.zeros((nd, BLOCK), BF16)
    for b in range(steps):
        loud = jnp.maximum(loud, jnp.abs(held[(lead + b) * nd : (lead + b + 1) * nd, :]))
    loud = jnp.maximum(jnp.max(loud.astype(F32), axis=1, keepdims=True), TINY)
    quiet = jnp.broadcast_to(TOP / loud, (nd, BLOCK))
    across = jnp.sum(jnp.where(row == lane, jnp.broadcast_to(loud, (nd, L)), 0.0), axis=0, keepdims=True)
    across = jnp.concatenate([across[:, :nd]] * groups, axis=1)
    scaled = rest[...] * across
    largest = jnp.max(jnp.max(jnp.abs(scaled), axis=0, keepdims=True), axis=1, keepdims=True)
    largest = jnp.maximum(largest, TINY)
    table8[...] = (scaled * (TOP / largest)).astype(FP8)
    back = largest * (1.0 / (TOP * TOP))

    def shrink(b):
        if b < steps:
            at = (lead + b) * nd
            held8[at : at + nd, :] = (held[at : at + nd, :].astype(F32) * quiet).astype(FP8)

    slots = diagonal.shape[0]
    count = steps + lead

    def product(v):
        half = groups // 2
        low = half if v + half <= lead else 0
        high = half if v + half >= lead + steps else groups
        rows, cols = slice((v + low) * nd, (v + high) * nd), slice(low * nd, high * nd)
        main = jnp.dot(table[:, cols], held[rows, :], preferred_element_type=F32)
        small = jnp.dot(table8[:, cols], held8[rows, :], preferred_element_type=F32)
        diagonal[v % slots] = main + small * back

    def add_diagonals(tiles, at):
        total = direct = None
        for b in range(0, L, 8):
            part = tiles[0][b : b + 8]
            for other in tiles[1:]:
                part += other[b : b + 8]
            part = pltpu.roll(part, b + 1, 1, stride=1, stride_axis=0)
            kept = jnp.where(lane8 > row8 + b, part, 0.0)
            total = part if total is None else total + part
            direct = kept if direct is None else direct + kept
        line[at] += direct
        line[at + 1] += total - direct

    def corner(v, down, across):
        return diagonal[v % slots, down * L : (down + 1) * L, across * L : (across + 1) * L]

    shrink(0)
    shrink(1)
    product(0)
    for v in range(count):
        shrink(v + 2)
        if v + 1 < count:
            product(v + 1)
        first = [corner(v, 0, 0)] + ([corner(v - 1, 1, 1)] if v else [])
        add_diagonals(first, 2 * v)
        add_diagonals([corner(v, 1, 0), corner(v, 0, 1)], 2 * v + 1)
        if v >= lead:
            for half in range(2):
                x = held[v * nd : (v + 1) * nd, half * L : (half + 1) * L]
                line[2 * (v - lead) + half] += (x.astype(F32) * last).reshape(nd // 8, 8, L).sum(0)
    add_diagonals([corner(count - 1, 1, 1)], 2 * count)
    out[0 : plan.out, :] = jnp.sum(line[0 : plan.out], axis=1)

    nb = plan.blocks
    pad = ((0, 0), (0, L - nb))
    target = jnp.pad(owner[...], pad) * TROWS + jnp.pad(tile_row[...], pad)
    kept = lax.broadcasted_iota(jnp.int32, (1, L), 1) < counts[0, 0]
    target = jnp.where(kept, target, -1)
    out[plan.out : plan.out + 8, :] = jnp.broadcast_to(target.astype(F32), (8, L))


def two_terms(x):
    high = x.astype(BF16)
    return high, (x - high.astype(F32)).astype(BF16)


def rows_of(target, first, count):
    row = lax.broadcasted_iota(jnp.int32, (count, target.shape[1]), 0).astype(F32) + first
    row = jnp.where(row < 0, -2.0, row)
    return (jnp.broadcast_to(target, row.shape) == row).astype(BF16)


def add_rows(picks, blocks):
    high, low = two_terms(blocks)
    both = jnp.dot(picks, jnp.concatenate([high, low], axis=1), preferred_element_type=F32)
    return both[:, :L] + both[:, L:]


def tile_rows_kernel(*refs, plan, reach):
    parts, (home, away) = refs[:-2], refs[-2:]
    nb, halo = plan.blocks, plan.reach
    me = lax.axis_index("tm")
    ext = TROWS + 2 * reach
    marks_at = ext + 2 * halo * len(parts)
    away[marks_at:, :] = jnp.full((away.shape[0] - marks_at, L), -1.0, F32)

    for k, ref in enumerate(parts):
        at = ext + 2 * halo * k
        away[at : at + halo, :] = ref[0:halo, :]
        away[at + halo : at + 2 * halo, :] = ref[halo + nb : plan.out, :]
        away[marks_at + k : marks_at + k + 1, :] = ref[plan.out : plan.out + 1, :]
    target = jnp.concatenate([ref[plan.out : plan.out + 1, 0:nb] for ref in parts], axis=1)
    blocks = jnp.concatenate([ref[halo : halo + nb, :] for ref in parts], axis=0)
    for out, tile in ((home, me), (away, jnp.bitwise_xor(me, 1))):
        out[0:ext, :] = add_rows(rows_of(target, (tile * TROWS - reach).astype(F32), ext), blocks)


def windows_kernel(*refs, plan, order, bands, reach):
    home, here, other, beam_rows, beam_cols, mixing, out, marks, tile = refs
    me = lax.axis_index("tm")
    mine = lax.axis_index("band") // 2
    nb, halo = plan.blocks, plan.reach
    ext = TROWS + 2 * reach
    after_rows = ext + 2 * halo * len(order)
    marks[...] = jnp.full_like(marks, -1.0)
    numbers = []
    for side, ref in enumerate((here, other)):
        for k, z in enumerate(order):
            t = jnp.bitwise_xor(me, 2 * z + side)
            marks[pl.ds(8 + t, 1), :] = ref[after_rows + k : after_rows + k + 1, :]
            numbers.append(t)
    targets = []
    for t in numbers:
        before = marks[pl.ds(7 + t, 1), :]
        after = marks[pl.ds(9 + t, 1), :]
        targets += [before[:, nb - halo : nb], after[:, 0:halo]]
    blocks = [here[ext:after_rows, :], other[ext:after_rows, :]]
    picks = rows_of(jnp.concatenate(targets, axis=1), (me * TROWS - reach).astype(F32), ext)
    tile[...] = home[...] + other[0:ext, :] + add_rows(picks, jnp.concatenate(blocks, axis=0))
    share = TROWS // bands
    wide = 2 * share + 2 * reach
    terms, taps = beam_rows.shape[1:]
    comps = mixing.shape[0]
    out[...] = jnp.zeros_like(out)
    pad = jnp.zeros((8, L - taps), F32)
    lane = lax.broadcasted_iota(jnp.int32, (8, L), 1)
    turn = jnp.where(lane < taps, taps - 1 - lane, lane)
    for h in range(bands // 2):
        start = pl.multiple_of(jnp.bitwise_xor(mine, h) * (2 * share), 8)
        out[h, 0:wide, :] = tile[pl.ds(start, wide), :]
        for k in range(terms):
            out[h, wide + k : wide + k + 1, 0:taps] = beam_rows[0, k : k + 1, :]
            profile = jnp.broadcast_to(beam_cols[0, k : k + 1, :], (8, taps))
            turned = jnp.take_along_axis(jnp.concatenate([profile, pad], axis=1), turn, axis=1)
            out[h, wide + terms + k : wide + terms + k + 1, :] = turned[0:1]
            for c in range(comps):
                at = wide + 2 * terms + c * terms + k
                out[h, at : at + 1, :] = jnp.broadcast_to(mixing[c, 0:1, k : k + 1], (1, L))


def dot3(a, b, dims):
    a0, a1 = two_terms(a)
    b0, b1 = two_terms(b)
    ka, kb = dims
    left = jnp.concatenate([a0, a0, a1], axis=ka)
    right = jnp.concatenate([b0, b1, b0], axis=kb)
    return lax.dot_general(left, right, (((ka,), (kb,)), ((), ())), preferred_element_type=F32)


def beam_kernel(*refs, windows, share, reach, terms, comps):
    ins, sofar, out = refs[:windows], refs[windows:-1], refs[-1]
    core = lax.rem(lax.axis_index("band"), 2)
    wide = 2 * share + 2 * reach
    need = share + 2 * reach
    x = lax.broadcasted_iota(jnp.int32, (L, L), 0)
    c_in = lax.broadcasted_iota(jnp.int32, (L, L), 1)
    near = jnp.abs(c_in - x) <= reach
    totals = [sofar[0][c, 0] if sofar else None for c in range(comps)]
    for ref in ins:
        for h in range(ref.shape[0]):
            rows = ref[h, pl.ds(pl.multiple_of(core * share, 8), need), :]
            mats = []
            for k in range(terms):
                spread = jnp.broadcast_to(ref[h, wide + k : wide + k + 1, :], (share, L))
                mats.append(pltpu.roll(spread, 0, 1, stride=1, stride_axis=0)[:, :need])
            rowed = dot3(jnp.concatenate(mats, axis=0), rows, (1, 0))
            for k in range(terms):
                at = wide + terms + k
                spread = jnp.broadcast_to(ref[h, at : at + 1, :], (L, L))
                cols = pltpu.roll(spread, L - reach, 1, stride=1, stride_axis=0)
                cols = jnp.where(near, cols, 0.0)
                beamed = dot3(rowed[k * share : (k + 1) * share], cols, (1, 0))
                for c in range(comps):
                    at = wide + 2 * terms + c * terms + k
                    part = beamed * ref[h, at : at + 1, :]
                    totals[c] = part if totals[c] is None else totals[c] + part
    for c in range(comps):
        out[c, 0] = totals[c]


def flip(x, axis, bits):
    count = lax.axis_size(axis)
    return lax.ppermute(x, axis, [(i, i ^ bits) for i in range(count)])


def on_device(
    tod, filter_taps, det_weights, owner, tile_row, block_counts, beam_rows, beam_cols, mixing
):
    detectors, samples = tod.shape[1:]
    taps = filter_taps.shape[2]
    plan = Plan(detectors, samples, taps)
    tms, bands = lax.axis_size("tm"), lax.axis_size("band")
    inner = 2
    outer = tms // inner
    terms, beam = beam_rows.shape[1:]
    reach = (beam - 1) // 2
    comps = mixing.shape[0]
    inputs = (det_weights, tod, filter_taps, owner[:, :, 0], tile_row)
    values = pl.pallas_call(
        functools.partial(filter_kernel, plan=plan),
        out_shape=jax.ShapeDtypeStruct((plan.out + 8, L), F32),
        in_specs=[ANY] * 6,
        out_specs=VMEM,
        scratch_shapes=[
            pltpu.VMEM((1, detectors), F32),
            pltpu.VMEM((detectors, taps), BF16),
            pltpu.VMEM((1, plan.blocks), jnp.int32),
            pltpu.VMEM((1, plan.blocks), jnp.int32),
            pltpu.SMEM((1, 1), jnp.int32),
            pltpu.VMEM(((plan.steps + 2 * plan.lead) * detectors, BLOCK), BF16),
            pltpu.VMEM(((plan.steps + 2 * plan.lead) * detectors, BLOCK), FP8),
            pltpu.VMEM((BLOCK, plan.groups * detectors), BF16),
            pltpu.VMEM((BLOCK, plan.groups * detectors), F32),
            pltpu.VMEM((BLOCK, plan.groups * detectors), FP8),
            pltpu.VMEM((plan.out + 8, 8, L), F32),
            pltpu.VMEM((3, BLOCK, BLOCK), F32),
            pltpu.SemaphoreType.DMA((plan.steps + 5,)),
        ],
        compiler_params=WHOLE,
        name="filter_blocks",
    )(*[pltpu.with_memory_space_constraint(v, pltpu.HBM) for v in inputs], block_counts)
    order = list(range(outer))
    parts = [flip(values, "tm", k * inner) if k else values for k in order]
    ext = TROWS + 2 * reach
    sent = ext + 2 * plan.reach * outer + -(-outer // 8) * 8
    home, away = pl.pallas_call(
        functools.partial(tile_rows_kernel, plan=plan, reach=reach),
        out_shape=(jax.ShapeDtypeStruct((ext, L), F32), jax.ShapeDtypeStruct((sent, L), F32)),
        in_specs=[VMEM] * outer,
        out_specs=(VMEM, VMEM),
        compiler_params=SMALL,
        name="tile_rows",
    )(*parts)
    other = flip(away, "tm", 1)
    share = TROWS // bands
    wide = 2 * share + 2 * reach
    extra = -(-(2 * terms + comps * terms) // 8) * 8
    windows = pl.pallas_call(
        functools.partial(windows_kernel, plan=plan, order=order, bands=bands, reach=reach),
        out_shape=jax.ShapeDtypeStruct((bands // 2, wide + extra, L), F32),
        in_specs=[VMEM] * 6,
        out_specs=VMEM,
        scratch_shapes=[pltpu.VMEM((16 + tms, L), F32), pltpu.VMEM((ext, L), F32)],
        compiler_params=SMALL,
        name="band_windows",
    )(home, away, other, beam_rows, beam_cols, mixing)
    own = windows[0:1]
    across = [flip(windows[h : h + 1], "band", 2 * h) for h in range(1, bands // 2)]
    smooth = functools.partial(beam_kernel, share=share, reach=reach, terms=terms, comps=comps)

    def add_beams(windows, *sofar):
        return pl.pallas_call(
            functools.partial(smooth, windows=len(windows)),
            out_shape=jax.ShapeDtypeStruct((comps, 1, share, L), F32),
            in_specs=[VMEM] * (len(windows) + len(sofar)),
            out_specs=VMEM,
            compiler_params=SMALL,
            cost_estimate=pl.CostEstimate(flops=10**9, bytes_accessed=10**6, transcendentals=0),
            name="smooth_and_mix",
        )(*windows, *sofar)

    result = add_beams([own])
    result = add_beams([flip(own, "band", 1)] + across, result)
    return add_beams([flip(window, "band", 1) for window in across], result)


def solution(mesh):
    placed = (
        P("band", None, "tm"),
        P("band", None, None),
        P("band", None),
        P("band", "tm", None),
        P("band", "tm"),
        P("band", "tm"),
        P("band", None, None),
        P("band", None, None),
        P(None, "band", None),
    )
    return jax.shard_map(
        on_device,
        mesh=mesh,
        in_specs=placed,
        out_specs=P(None, "tm", "band", None),
        check_vma=False,
    )
```

```python
import functools

import jax
import jax.numpy as jnp
from jax import lax
from jax.experimental import pallas as pl
from jax.experimental.pallas import tpu as pltpu
from jax.sharding import PartitionSpec as P

L = 128
TROWS = 128
BLOCK = 256
VMEM = pl.BlockSpec(memory_space=pltpu.VMEM)
ANY = pl.BlockSpec(memory_space=pl.ANY)
SMALL = pltpu.CompilerParams(vmem_limit_bytes=32 * 2**20)
WHOLE = pltpu.CompilerParams(vmem_limit_bytes=48 * 2**20)
F32, BF16, FP8 = jnp.float32, jnp.bfloat16, jnp.float8_e4m3fn
TOP = 256.0
TINY = 1e-30


class Plan:
    def __init__(self, detectors, samples, taps):
        self.detectors, self.samples, self.taps = detectors, samples, taps
        self.groups = (taps - 1) // BLOCK
        self.steps = samples // BLOCK
        self.lead = self.groups - 1
        self.blocks = samples // L
        self.reach = (taps - 1) // 2 // L
        self.out = self.blocks + 2 * self.reach


def filter_kernel(
    weights_in, tod, taps_in, owner_in, row_in, counts_in,
    out, weights, taps, owner, tile_row, counts, held, held8, table, rest, table8, line, diagonal, sems, *, plan
):
    nd, steps, lead, groups = plan.detectors, plan.steps, plan.lead, plan.groups
    small = [
        pltpu.make_async_copy(src, dst, sems.at[steps + i])
        for i, (src, dst) in enumerate(
            ((taps_in.at[0], taps), (weights_in, weights), (owner_in, owner), (row_in, tile_row), (counts_in, counts))
        )
    ]
    big = [
        pltpu.make_async_copy(
            tod.at[0, :, b * BLOCK : (b + 1) * BLOCK], held.at[(lead + b) * nd : (lead + b + 1) * nd, :], sems.at[b]
        )
        for b in range(steps)
    ]
    for copy in small + big:
        copy.start()
    held[0 : lead * nd, :] = jnp.zeros((lead * nd, BLOCK), BF16)
    held[(lead + steps) * nd :, :] = jnp.zeros((lead * nd, BLOCK), BF16)
    held8[0 : lead * nd, :] = jnp.zeros((lead * nd, BLOCK), FP8)
    held8[(lead + steps) * nd :, :] = jnp.zeros((lead * nd, BLOCK), FP8)
    line[...] = jnp.zeros_like(line)
    row = lax.broadcasted_iota(jnp.int32, (nd, L), 0)
    lane = lax.broadcasted_iota(jnp.int32, (nd, L), 1)
    for copy in small:
        copy.wait()
    spread = jnp.broadcast_to(jnp.pad(weights[...], ((0, 0), (0, L - nd))), (nd, L))
    column = jnp.sum(jnp.where(row == lane, spread, 0.0), axis=1, keepdims=True)
    for pair in range(groups // 2):
        for half in range(2):
            parts = []
            for j in (2 * pair, 2 * pair + 1):
                start = j * BLOCK + half * L
                part = taps[:, start : start + L].astype(F32) * column
                parts.append(jnp.take_along_axis(part, L - 1 - lane, axis=1))
            turned = jnp.concatenate(parts, axis=0).T
            high = turned.astype(BF16)
            at = (1 - half) * L
            table[at : at + L, pair * L : (pair + 1) * L] = high
            rest[at : at + L, pair * L : (pair + 1) * L] = turned - high.astype(F32)
    last = jnp.broadcast_to(taps[:, groups * BLOCK : groups * BLOCK + 1].astype(F32) * column, (nd, L))
    row8 = lax.broadcasted_iota(jnp.int32, (8, L), 0)
    lane8 = lax.broadcasted_iota(jnp.int32, (8, L), 1)
    for copy in big:
        copy.wait()

    loud = jnp.zeros((nd, BLOCK), BF16)
    for b in range(steps):
        loud = jnp.maximum(loud, jnp.abs(held[(lead + b) * nd : (lead + b + 1) * nd, :]))
    loud = jnp.maximum(jnp.max(loud.astype(F32), axis=1, keepdims=True), TINY)
    quiet = jnp.broadcast_to(TOP / loud, (nd, BLOCK))
    across = jnp.sum(jnp.where(row == lane, jnp.broadcast_to(loud, (nd, L)), 0.0), axis=0, keepdims=True)
    across = jnp.concatenate([across[:, :nd]] * groups, axis=1)
    scaled = rest[...] * across
    largest = jnp.max(jnp.max(jnp.abs(scaled), axis=0, keepdims=True), axis=1, keepdims=True)
    largest = jnp.maximum(largest, TINY)
    table8[...] = (scaled * (TOP / largest)).astype(FP8)
    back = largest * (1.0 / (TOP * TOP))

    def shrink(b):
        if b < steps:
            at = (lead + b) * nd
            held8[at : at + nd, :] = (held[at : at + nd, :].astype(F32) * quiet).astype(FP8)

    slots = diagonal.shape[0]
    count = steps + lead

    def product(v):
        half = groups // 2
        low = half if v + half <= lead else 0
        high = half if v + half >= lead + steps else groups
        rows, cols = slice((v + low) * nd, (v + high) * nd), slice(low * nd, high * nd)
        main = jnp.dot(table[:, cols], held[rows, :], preferred_element_type=F32)
        small = jnp.dot(table8[:, cols], held8[rows, :], preferred_element_type=F32)
        diagonal[v % slots] = main + small * back

    def add_diagonals(tiles, at):
        total = direct = None
        for b in range(0, L, 8):
            part = tiles[0][b : b + 8]
            for other in tiles[1:]:
                part += other[b : b + 8]
            part = pltpu.roll(part, b + 1, 1, stride=1, stride_axis=0)
            kept = jnp.where(lane8 > row8 + b, part, 0.0)
            total = part if total is None else total + part
            direct = kept if direct is None else direct + kept
        line[at] += direct
        line[at + 1] += total - direct

    def corner(v, down, across):
        return diagonal[v % slots, down * L : (down + 1) * L, across * L : (across + 1) * L]

    shrink(0)
    shrink(1)
    product(0)
    for v in range(count):
        shrink(v + 2)
        if v + 1 < count:
            product(v + 1)
        first = [corner(v, 0, 0)] + ([corner(v - 1, 1, 1)] if v else [])
        add_diagonals(first, 2 * v)
        add_diagonals([corner(v, 1, 0), corner(v, 0, 1)], 2 * v + 1)
        if v >= lead:
            for half in range(2):
                x = held[v * nd : (v + 1) * nd, half * L : (half + 1) * L]
                line[2 * (v - lead) + half] += (x.astype(F32) * last).reshape(nd // 8, 8, L).sum(0)
    add_diagonals([corner(count - 1, 1, 1)], 2 * count)
    out[0 : plan.out, :] = jnp.sum(line[0 : plan.out], axis=1)

    nb = plan.blocks
    pad = ((0, 0), (0, L - nb))
    target = jnp.pad(owner[...], pad) * TROWS + jnp.pad(tile_row[...], pad)
    kept = lax.broadcasted_iota(jnp.int32, (1, L), 1) < counts[0, 0]
    target = jnp.where(kept, target, -1)
    out[plan.out : plan.out + 8, :] = jnp.broadcast_to(target.astype(F32), (8, L))


def two_terms(x):
    high = x.astype(BF16)
    return high, (x - high.astype(F32)).astype(BF16)


def rows_of(target, first, count):
    row = lax.broadcasted_iota(jnp.int32, (count, target.shape[1]), 0).astype(F32) + first
    row = jnp.where(row < 0, -2.0, row)
    return (jnp.broadcast_to(target, row.shape) == row).astype(BF16)


def add_rows(picks, blocks):
    high, low = two_terms(blocks)
    both = jnp.dot(picks, jnp.concatenate([high, low], axis=1), preferred_element_type=F32)
    return both[:, :L] + both[:, L:]


def tile_rows_kernel(*refs, plan, reach):
    parts, (home, away) = refs[:-2], refs[-2:]
    nb, halo = plan.blocks, plan.reach
    me = lax.axis_index("tm")
    ext = TROWS + 2 * reach
    marks_at = ext + 2 * halo * len(parts)
    away[marks_at:, :] = jnp.full((away.shape[0] - marks_at, L), -1.0, F32)

    for k, ref in enumerate(parts):
        at = ext + 2 * halo * k
        away[at : at + halo, :] = ref[0:halo, :]
        away[at + halo : at + 2 * halo, :] = ref[halo + nb : plan.out, :]
        away[marks_at + k : marks_at + k + 1, :] = ref[plan.out : plan.out + 1, :]
    target = jnp.concatenate([ref[plan.out : plan.out + 1, 0:nb] for ref in parts], axis=1)
    blocks = jnp.concatenate([ref[halo : halo + nb, :] for ref in parts], axis=0)
    for out, tile in ((home, me), (away, jnp.bitwise_xor(me, 1))):
        out[0:ext, :] = add_rows(rows_of(target, (tile * TROWS - reach).astype(F32), ext), blocks)


def windows_kernel(*refs, plan, order, bands, reach):
    home, here, other, beam_rows, beam_cols, mixing, out, marks, tile = refs
    me = lax.axis_index("tm")
    mine = lax.axis_index("band")
    nb, halo = plan.blocks, plan.reach
    ext = TROWS + 2 * reach
    after_rows = ext + 2 * halo * len(order)
    marks[...] = jnp.full_like(marks, -1.0)
    numbers = []
    for side, ref in enumerate((here, other)):
        for k, z in enumerate(order):
            t = jnp.bitwise_xor(me, 2 * z + side)
            marks[pl.ds(8 + t, 1), :] = ref[after_rows + k : after_rows + k + 1, :]
            numbers.append(t)
    targets = []
    for t in numbers:
        before = marks[pl.ds(7 + t, 1), :]
        after = marks[pl.ds(9 + t, 1), :]
        targets += [before[:, nb - halo : nb], after[:, 0:halo]]
    blocks = [here[ext:after_rows, :], other[ext:after_rows, :]]
    picks = rows_of(jnp.concatenate(targets, axis=1), (me * TROWS - reach).astype(F32), ext)
    tile[...] = home[...] + other[0:ext, :] + add_rows(picks, jnp.concatenate(blocks, axis=0))
    share = TROWS // bands
    wide = share + 2 * reach
    terms, taps = beam_rows.shape[1:]
    comps = mixing.shape[0]
    out[...] = jnp.zeros_like(out)
    pad = jnp.zeros((8, L - taps), F32)
    lane = lax.broadcasted_iota(jnp.int32, (8, L), 1)
    turn = jnp.where(lane < taps, taps - 1 - lane, lane)
    for h in range(bands):
        start = pl.multiple_of(jnp.bitwise_xor(mine, h) * share, 8)
        out[h, 0:wide, :] = tile[pl.ds(start, wide), :]
        for k in range(terms):
            out[h, wide + k : wide + k + 1, 0:taps] = beam_rows[0, k : k + 1, :]
            profile = jnp.broadcast_to(beam_cols[0, k : k + 1, :], (8, taps))
            turned = jnp.take_along_axis(jnp.concatenate([profile, pad], axis=1), turn, axis=1)
            out[h, wide + terms + k : wide + terms + k + 1, :] = turned[0:1]
            for c in range(comps):
                at = wide + 2 * terms + c * terms + k
                out[h, at : at + 1, :] = jnp.broadcast_to(mixing[c, 0:1, k : k + 1], (1, L))


def dot3(a, b, dims):
    a0, a1 = two_terms(a)
    b0, b1 = two_terms(b)
    ka, kb = dims
    left = jnp.concatenate([a0, a0, a1], axis=ka)
    right = jnp.concatenate([b0, b1, b0], axis=kb)
    return lax.dot_general(left, right, (((ka,), (kb,)), ((), ())), preferred_element_type=F32)


def beam_kernel(*refs, windows, share, reach, terms, comps):
    ins, sofar, out = refs[:windows], refs[windows:-1], refs[-1]
    wide = share + 2 * reach
    x = lax.broadcasted_iota(jnp.int32, (L, L), 0)
    c_in = lax.broadcasted_iota(jnp.int32, (L, L), 1)
    near = jnp.abs(c_in - x) <= reach
    totals = [sofar[0][c, 0] if sofar else None for c in range(comps)]
    for ref in ins:
        for h in range(ref.shape[0]):
            rows = ref[h, 0:wide, :]
            mats = []
            for k in range(terms):
                spread = jnp.broadcast_to(ref[h, wide + k : wide + k + 1, :], (share, L))
                mats.append(pltpu.roll(spread, 0, 1, stride=1, stride_axis=0)[:, :wide])
            rowed = dot3(jnp.concatenate(mats, axis=0), rows, (1, 0))
            for k in range(terms):
                at = wide + terms + k
                spread = jnp.broadcast_to(ref[h, at : at + 1, :], (L, L))
                cols = pltpu.roll(spread, L - reach, 1, stride=1, stride_axis=0)
                cols = jnp.where(near, cols, 0.0)
                beamed = dot3(rowed[k * share : (k + 1) * share], cols, (1, 0))
                for c in range(comps):
                    at = wide + 2 * terms + c * terms + k
                    part = beamed * ref[h, at : at + 1, :]
                    totals[c] = part if totals[c] is None else totals[c] + part
    for c in range(comps):
        out[c, 0] = totals[c]


def flip(x, axis, bits):
    count = lax.axis_size(axis)
    return lax.ppermute(x, axis, [(i, i ^ bits) for i in range(count)])


def on_device(
    tod, filter_taps, det_weights, owner, tile_row, block_counts, beam_rows, beam_cols, mixing
):
    detectors, samples = tod.shape[1:]
    taps = filter_taps.shape[2]
    plan = Plan(detectors, samples, taps)
    tms, bands = lax.axis_size("tm"), lax.axis_size("band")
    inner = 2
    outer = tms // inner
    terms, beam = beam_rows.shape[1:]
    reach = (beam - 1) // 2
    comps = mixing.shape[0]
    inputs = (det_weights, tod, filter_taps, owner[:, :, 0], tile_row)
    values = pl.pallas_call(
        functools.partial(filter_kernel, plan=plan),
        out_shape=jax.ShapeDtypeStruct((plan.out + 8, L), F32),
        in_specs=[ANY] * 6,
        out_specs=VMEM,
        scratch_shapes=[
            pltpu.VMEM((1, detectors), F32),
            pltpu.VMEM((detectors, taps), BF16),
            pltpu.VMEM((1, plan.blocks), jnp.int32),
            pltpu.VMEM((1, plan.blocks), jnp.int32),
            pltpu.SMEM((1, 1), jnp.int32),
            pltpu.VMEM(((plan.steps + 2 * plan.lead) * detectors, BLOCK), BF16),
            pltpu.VMEM(((plan.steps + 2 * plan.lead) * detectors, BLOCK), FP8),
            pltpu.VMEM((BLOCK, plan.groups * detectors), BF16),
            pltpu.VMEM((BLOCK, plan.groups * detectors), F32),
            pltpu.VMEM((BLOCK, plan.groups * detectors), FP8),
            pltpu.VMEM((plan.out + 8, 8, L), F32),
            pltpu.VMEM((3, BLOCK, BLOCK), F32),
            pltpu.SemaphoreType.DMA((plan.steps + 5,)),
        ],
        compiler_params=WHOLE,
        name="filter_blocks",
    )(*[pltpu.with_memory_space_constraint(v, pltpu.HBM) for v in inputs], block_counts)
    order = list(range(outer))
    parts = [flip(values, "tm", k * inner) if k else values for k in order]
    ext = TROWS + 2 * reach
    sent = ext + 2 * plan.reach * outer + -(-outer // 8) * 8
    home, away = pl.pallas_call(
        functools.partial(tile_rows_kernel, plan=plan, reach=reach),
        out_shape=(jax.ShapeDtypeStruct((ext, L), F32), jax.ShapeDtypeStruct((sent, L), F32)),
        in_specs=[VMEM] * outer,
        out_specs=(VMEM, VMEM),
        compiler_params=SMALL,
        name="tile_rows",
    )(*parts)
    other = flip(away, "tm", 1)
    share = TROWS // bands
    wide = share + 2 * reach
    extra = -(-(2 * terms + comps * terms) // 8) * 8
    windows = pl.pallas_call(
        functools.partial(windows_kernel, plan=plan, order=order, bands=bands, reach=reach),
        out_shape=jax.ShapeDtypeStruct((bands, wide + extra, L), F32),
        in_specs=[VMEM] * 6,
        out_specs=VMEM,
        scratch_shapes=[pltpu.VMEM((16 + tms, L), F32), pltpu.VMEM((ext, L), F32)],
        compiler_params=SMALL,
        name="band_windows",
    )(home, away, other, beam_rows, beam_cols, mixing)
    half = bands // 2
    sent = {h: flip(windows[h : h + 1], "band", h) for h in list(range(half, bands)) + list(range(1, half))}
    smooth = functools.partial(beam_kernel, share=share, reach=reach, terms=terms, comps=comps)

    def add_beams(windows, *sofar):
        return pl.pallas_call(
            functools.partial(smooth, windows=len(windows)),
            out_shape=jax.ShapeDtypeStruct((comps, 1, share, L), F32),
            in_specs=[VMEM] * (len(windows) + len(sofar)),
            out_specs=VMEM,
            compiler_params=SMALL,
            cost_estimate=pl.CostEstimate(flops=10**9, bytes_accessed=10**6, transcendentals=0),
            name="smooth_and_mix",
        )(*windows, *sofar)

    result = add_beams([windows[0:1]] + [sent[h] for h in range(1, half)])
    result = add_beams([sent[half]], result)
    return add_beams([sent[h] for h in range(half + 1, bands)], result)


def solution(mesh):
    placed = (
        P("band", None, "tm"),
        P("band", None, None),
        P("band", None),
        P("band", "tm", None),
        P("band", "tm"),
        P("band", "tm"),
        P("band", None, None),
        P("band", None, None),
        P(None, "band", None),
    )
    return jax.shard_map(
        on_device,
        mesh=mesh,
        in_specs=placed,
        out_specs=P(None, "tm", "band", None),
        check_vma=False,
    )
```

```python
import functools

import jax
import jax.numpy as jnp
from jax import lax
from jax.experimental import pallas as pl
from jax.experimental.pallas import tpu as pltpu
from jax.sharding import PartitionSpec as P

L = 128
TROWS = 128
BLOCK = 256
VMEM = pl.BlockSpec(memory_space=pltpu.VMEM)
ANY = pl.BlockSpec(memory_space=pl.ANY)
SMALL = pltpu.CompilerParams(vmem_limit_bytes=32 * 2**20)
WHOLE = pltpu.CompilerParams(vmem_limit_bytes=48 * 2**20)
F32, BF16, FP8 = jnp.float32, jnp.bfloat16, jnp.float8_e4m3fn
TOP = 256.0
TINY = 1e-30


class Plan:
    def __init__(self, detectors, samples, taps):
        self.detectors, self.samples, self.taps = detectors, samples, taps
        self.groups = (taps - 1) // BLOCK
        self.steps = samples // BLOCK
        self.lead = self.groups - 1
        self.blocks = samples // L
        self.reach = (taps - 1) // 2 // L
        self.out = self.blocks + 2 * self.reach


def filter_kernel(
    weights_in, tod, taps_in, owner_in, row_in, counts_in,
    out, weights, taps, owner, tile_row, counts, held, held8, table, rest, table8, line, diagonal, sems, *, plan
):
    nd, steps, lead, groups = plan.detectors, plan.steps, plan.lead, plan.groups
    small = [
        pltpu.make_async_copy(src, dst, sems.at[steps + i])
        for i, (src, dst) in enumerate(
            ((taps_in.at[0], taps), (weights_in, weights), (owner_in, owner), (row_in, tile_row), (counts_in, counts))
        )
    ]
    big = [
        pltpu.make_async_copy(
            tod.at[0, :, b * BLOCK : (b + 1) * BLOCK], held.at[(lead + b) * nd : (lead + b + 1) * nd, :], sems.at[b]
        )
        for b in range(steps)
    ]
    for copy in small + big:
        copy.start()
    held[0 : lead * nd, :] = jnp.zeros((lead * nd, BLOCK), BF16)
    held[(lead + steps) * nd :, :] = jnp.zeros((lead * nd, BLOCK), BF16)
    held8[0 : lead * nd, :] = jnp.zeros((lead * nd, BLOCK), FP8)
    held8[(lead + steps) * nd :, :] = jnp.zeros((lead * nd, BLOCK), FP8)
    line[...] = jnp.zeros_like(line)
    row = lax.broadcasted_iota(jnp.int32, (nd, L), 0)
    lane = lax.broadcasted_iota(jnp.int32, (nd, L), 1)
    for copy in small:
        copy.wait()
    spread = jnp.broadcast_to(jnp.pad(weights[...], ((0, 0), (0, L - nd))), (nd, L))
    column = jnp.sum(jnp.where(row == lane, spread, 0.0), axis=1, keepdims=True)
    for pair in range(groups // 2):
        for half in range(2):
            parts = []
            for j in (2 * pair, 2 * pair + 1):
                start = j * BLOCK + half * L
                part = taps[:, start : start + L].astype(F32) * column
                parts.append(jnp.take_along_axis(part, L - 1 - lane, axis=1))
            turned = jnp.concatenate(parts, axis=0).T
            high = turned.astype(BF16)
            at = (1 - half) * L
            table[at : at + L, pair * L : (pair + 1) * L] = high
            rest[at : at + L, pair * L : (pair + 1) * L] = turned - high.astype(F32)
    left = jnp.maximum(jnp.max(jnp.abs(rest[...]), axis=0, keepdims=True), TINY)
    most = left[:, :nd]
    for j in range(1, groups):
        most = jnp.maximum(most, left[:, j * nd : (j + 1) * nd])
    table8[...] = (rest[...] * jnp.concatenate([TOP / most] * groups, axis=1)).astype(FP8)
    most = jnp.broadcast_to(jnp.pad(most, ((0, 0), (0, L - nd))), (nd, L))
    most = jnp.sum(jnp.where(row == lane, most, 0.0), axis=1, keepdims=True)
    last = jnp.broadcast_to(taps[:, groups * BLOCK : groups * BLOCK + 1].astype(F32) * column, (nd, L))
    row8 = lax.broadcasted_iota(jnp.int32, (8, L), 0)
    lane8 = lax.broadcasted_iota(jnp.int32, (8, L), 1)
    for copy in big:
        copy.wait()

    loud = jnp.zeros((nd, BLOCK), BF16)
    for b in range(steps):
        loud = jnp.maximum(loud, jnp.abs(held[(lead + b) * nd : (lead + b + 1) * nd, :]))
    loud = jnp.max(loud.astype(F32), axis=1, keepdims=True) * most
    largest = jnp.maximum(jnp.max(loud, axis=0, keepdims=True), TINY)
    quiet = jnp.broadcast_to(most * (TOP / largest), (nd, BLOCK))
    back = largest * (1.0 / (TOP * TOP))

    def shrink(b):
        if b < steps:
            at = (lead + b) * nd
            held8[at : at + nd, :] = (held[at : at + nd, :].astype(F32) * quiet).astype(FP8)

    slots = diagonal.shape[0]
    count = steps + lead

    def product(v):
        half = groups // 2
        low = half if v + half <= lead else 0
        high = half if v + half >= lead + steps else groups
        rows, cols = slice((v + low) * nd, (v + high) * nd), slice(low * nd, high * nd)
        main = jnp.dot(table[:, cols], held[rows, :], preferred_element_type=F32)
        small = jnp.dot(table8[:, cols], held8[rows, :], preferred_element_type=F32)
        diagonal[v % slots] = main + small * back

    def add_diagonals(tiles, at):
        total = direct = None
        for b in range(0, L, 8):
            part = tiles[0][b : b + 8]
            for other in tiles[1:]:
                part += other[b : b + 8]
            part = pltpu.roll(part, b + 1, 1, stride=1, stride_axis=0)
            kept = jnp.where(lane8 > row8 + b, part, 0.0)
            total = part if total is None else total + part
            direct = kept if direct is None else direct + kept
        line[at] += direct
        line[at + 1] += total - direct

    def corner(v, down, across):
        return diagonal[v % slots, down * L : (down + 1) * L, across * L : (across + 1) * L]

    shrink(0)
    shrink(1)
    product(0)
    for v in range(count):
        shrink(v + 2)
        if v + 1 < count:
            product(v + 1)
        first = [corner(v, 0, 0)] + ([corner(v - 1, 1, 1)] if v else [])
        add_diagonals(first, 2 * v)
        add_diagonals([corner(v, 1, 0), corner(v, 0, 1)], 2 * v + 1)
        if v >= lead:
            for half in range(2):
                x = held[v * nd : (v + 1) * nd, half * L : (half + 1) * L]
                line[2 * (v - lead) + half] += (x.astype(F32) * last).reshape(nd // 8, 8, L).sum(0)
    add_diagonals([corner(count - 1, 1, 1)], 2 * count)
    out[0 : plan.out, :] = jnp.sum(line[0 : plan.out], axis=1)

    nb = plan.blocks
    pad = ((0, 0), (0, L - nb))
    target = jnp.pad(owner[...], pad) * TROWS + jnp.pad(tile_row[...], pad)
    kept = lax.broadcasted_iota(jnp.int32, (1, L), 1) < counts[0, 0]
    target = jnp.where(kept, target, -1)
    out[plan.out : plan.out + 8, :] = jnp.broadcast_to(target.astype(F32), (8, L))


def two_terms(x):
    high = x.astype(BF16)
    return high, (x - high.astype(F32)).astype(BF16)


def rows_of(target, first, count):
    row = lax.broadcasted_iota(jnp.int32, (count, target.shape[1]), 0).astype(F32) + first
    row = jnp.where(row < 0, -2.0, row)
    return (jnp.broadcast_to(target, row.shape) == row).astype(BF16)


def add_rows(picks, blocks):
    high, low = two_terms(blocks)
    both = jnp.dot(picks, jnp.concatenate([high, low], axis=1), preferred_element_type=F32)
    return both[:, :L] + both[:, L:]


def tile_rows_kernel(*refs, plan, reach):
    parts, (home, away) = refs[:-2], refs[-2:]
    nb, halo = plan.blocks, plan.reach
    me = lax.axis_index("tm")
    ext = TROWS + 2 * reach
    marks_at = ext + 2 * halo * len(parts)
    away[marks_at:, :] = jnp.full((away.shape[0] - marks_at, L), -1.0, F32)

    for k, ref in enumerate(parts):
        at = ext + 2 * halo * k
        away[at : at + halo, :] = ref[0:halo, :]
        away[at + halo : at + 2 * halo, :] = ref[halo + nb : plan.out, :]
        away[marks_at + k : marks_at + k + 1, :] = ref[plan.out : plan.out + 1, :]
    target = jnp.concatenate([ref[plan.out : plan.out + 1, 0:nb] for ref in parts], axis=1)
    blocks = jnp.concatenate([ref[halo : halo + nb, :] for ref in parts], axis=0)
    for out, tile in ((home, me), (away, jnp.bitwise_xor(me, 1))):
        out[0:ext, :] = add_rows(rows_of(target, (tile * TROWS - reach).astype(F32), ext), blocks)


def windows_kernel(*refs, plan, order, bands, reach):
    home, here, other, beam_rows, beam_cols, mixing, out, marks, tile = refs
    me = lax.axis_index("tm")
    mine = lax.axis_index("band")
    nb, halo = plan.blocks, plan.reach
    ext = TROWS + 2 * reach
    after_rows = ext + 2 * halo * len(order)
    marks[...] = jnp.full_like(marks, -1.0)
    numbers = []
    for side, ref in enumerate((here, other)):
        for k, z in enumerate(order):
            t = jnp.bitwise_xor(me, 2 * z + side)
            marks[pl.ds(8 + t, 1), :] = ref[after_rows + k : after_rows + k + 1, :]
            numbers.append(t)
    targets = []
    for t in numbers:
        before = marks[pl.ds(7 + t, 1), :]
        after = marks[pl.ds(9 + t, 1), :]
        targets += [before[:, nb - halo : nb], after[:, 0:halo]]
    blocks = [here[ext:after_rows, :], other[ext:after_rows, :]]
    picks = rows_of(jnp.concatenate(targets, axis=1), (me * TROWS - reach).astype(F32), ext)
    tile[...] = home[...] + other[0:ext, :] + add_rows(picks, jnp.concatenate(blocks, axis=0))
    share = TROWS // bands
    wide = share + 2 * reach
    terms, taps = beam_rows.shape[1:]
    comps = mixing.shape[0]
    out[...] = jnp.zeros_like(out)
    pad = jnp.zeros((8, L - taps), F32)
    lane = lax.broadcasted_iota(jnp.int32, (8, L), 1)
    turn = jnp.where(lane < taps, taps - 1 - lane, lane)
    for h in range(bands):
        start = pl.multiple_of(jnp.bitwise_xor(mine, h) * share, 8)
        out[h, 0:wide, :] = tile[pl.ds(start, wide), :]
        for k in range(terms):
            out[h, wide + k : wide + k + 1, 0:taps] = beam_rows[0, k : k + 1, :]
            profile = jnp.broadcast_to(beam_cols[0, k : k + 1, :], (8, taps))
            turned = jnp.take_along_axis(jnp.concatenate([profile, pad], axis=1), turn, axis=1)
            out[h, wide + terms + k : wide + terms + k + 1, :] = turned[0:1]
        for c in range(comps):
            at = wide + 2 * terms
            out[h, at : at + 1, c * terms : (c + 1) * terms] = mixing[c, 0:1, :]


def dot3(a, b, dims):
    a0, a1 = two_terms(a)
    b0, b1 = two_terms(b)
    ka, kb = dims
    left = jnp.concatenate([a0, a0, a1], axis=ka)
    right = jnp.concatenate([b0, b1, b0], axis=kb)
    return lax.dot_general(left, right, (((ka,), (kb,)), ((), ())), preferred_element_type=F32)


def beam_kernel(*refs, windows, share, reach, terms, comps, last):
    if last:
        refs, (stage, sems) = refs[:-2], refs[-2:]
    ins, sofar, out = refs[:windows], refs[windows:-1], refs[-1]
    wide = share + 2 * reach
    x = lax.broadcasted_iota(jnp.int32, (L, L), 0)
    c_in = lax.broadcasted_iota(jnp.int32, (L, L), 1)
    near = jnp.abs(c_in - x) <= reach
    totals = [sofar[0][c, 0] if sofar else None for c in range(comps)]
    for ref in ins:
        for h in range(ref.shape[0]):
            rows = ref[h, 0:wide, :]
            mats = []
            for k in range(terms):
                spread = jnp.broadcast_to(ref[h, wide + k : wide + k + 1, :], (share, L))
                mats.append(pltpu.roll(spread, 0, 1, stride=1, stride_axis=0)[:, :wide])
            rowed = dot3(jnp.concatenate(mats, axis=0), rows, (1, 0))
            for k in range(terms):
                at = wide + terms + k
                spread = jnp.broadcast_to(ref[h, at : at + 1, :], (L, L))
                cols = pltpu.roll(spread, L - reach, 1, stride=1, stride_axis=0)
                cols = jnp.where(near, cols, 0.0)
                beamed = dot3(rowed[k * share : (k + 1) * share], cols, (1, 0))
                for c in range(comps):
                    at, lane = wide + 2 * terms, c * terms + k
                    part = beamed * ref[h, at : at + 1, lane : lane + 1]
                    totals[c] = part if totals[c] is None else totals[c] + part
    if not last:
        for c in range(comps):
            out[c, 0] = totals[c]
        return
    copies = [pltpu.make_async_copy(stage.at[c], out.at[c, 0], sems.at[c]) for c in range(comps)]
    for c in range(comps):
        stage[c] = totals[c]
        copies[c].start()
    for copy in copies:
        copy.wait()


def flip(x, axis, bits):
    count = lax.axis_size(axis)
    return lax.ppermute(x, axis, [(i, i ^ bits) for i in range(count)])


def on_device(
    tod, filter_taps, det_weights, owner, tile_row, block_counts, beam_rows, beam_cols, mixing
):
    detectors, samples = tod.shape[1:]
    taps = filter_taps.shape[2]
    plan = Plan(detectors, samples, taps)
    tms, bands = lax.axis_size("tm"), lax.axis_size("band")
    inner = 2
    outer = tms // inner
    terms, beam = beam_rows.shape[1:]
    reach = (beam - 1) // 2
    comps = mixing.shape[0]
    inputs = (det_weights, tod, filter_taps, owner[:, :, 0], tile_row)
    values = pl.pallas_call(
        functools.partial(filter_kernel, plan=plan),
        out_shape=jax.ShapeDtypeStruct((plan.out + 8, L), F32),
        in_specs=[ANY] * 6,
        out_specs=VMEM,
        scratch_shapes=[
            pltpu.VMEM((1, detectors), F32),
            pltpu.VMEM((detectors, taps), BF16),
            pltpu.VMEM((1, plan.blocks), jnp.int32),
            pltpu.VMEM((1, plan.blocks), jnp.int32),
            pltpu.SMEM((1, 1), jnp.int32),
            pltpu.VMEM(((plan.steps + 2 * plan.lead) * detectors, BLOCK), BF16),
            pltpu.VMEM(((plan.steps + 2 * plan.lead) * detectors, BLOCK), FP8),
            pltpu.VMEM((BLOCK, plan.groups * detectors), BF16),
            pltpu.VMEM((BLOCK, plan.groups * detectors), F32),
            pltpu.VMEM((BLOCK, plan.groups * detectors), FP8),
            pltpu.VMEM((plan.out + 8, 8, L), F32),
            pltpu.VMEM((3, BLOCK, BLOCK), F32),
            pltpu.SemaphoreType.DMA((plan.steps + 5,)),
        ],
        compiler_params=WHOLE,
        name="filter_blocks",
    )(*[pltpu.with_memory_space_constraint(v, pltpu.HBM) for v in inputs], block_counts)
    order = list(range(outer))
    parts = [flip(values, "tm", k * inner) if k else values for k in order]
    ext = TROWS + 2 * reach
    sent = ext + 2 * plan.reach * outer + -(-outer // 8) * 8
    home, away = pl.pallas_call(
        functools.partial(tile_rows_kernel, plan=plan, reach=reach),
        out_shape=(jax.ShapeDtypeStruct((ext, L), F32), jax.ShapeDtypeStruct((sent, L), F32)),
        in_specs=[VMEM] * outer,
        out_specs=(VMEM, VMEM),
        compiler_params=SMALL,
        name="tile_rows",
    )(*parts)
    other = flip(away, "tm", 1)
    share = TROWS // bands
    wide = share + 2 * reach
    extra = -(-(2 * terms + 1) // 8) * 8
    windows = pl.pallas_call(
        functools.partial(windows_kernel, plan=plan, order=order, bands=bands, reach=reach),
        out_shape=jax.ShapeDtypeStruct((bands, wide + extra, L), F32),
        in_specs=[VMEM] * 6,
        out_specs=VMEM,
        scratch_shapes=[pltpu.VMEM((16 + tms, L), F32), pltpu.VMEM((ext, L), F32)],
        compiler_params=SMALL,
        name="band_windows",
    )(home, away, other, beam_rows, beam_cols, mixing)
    half = bands // 2
    sent = {h: flip(windows[h : h + 1], "band", h) for h in list(range(half, bands)) + list(range(1, half))}
    smooth = functools.partial(beam_kernel, share=share, reach=reach, terms=terms, comps=comps)

    def add_beams(windows, *sofar, last=False):
        return pl.pallas_call(
            functools.partial(smooth, windows=len(windows), last=last),
            out_shape=jax.ShapeDtypeStruct((comps, 1, share, L), F32),
            in_specs=[VMEM] * (len(windows) + len(sofar)),
            out_specs=ANY if last else VMEM,
            scratch_shapes=[pltpu.VMEM((comps, share, L), F32), pltpu.SemaphoreType.DMA((comps,))] if last else [],
            compiler_params=SMALL,
            cost_estimate=pl.CostEstimate(flops=10**9, bytes_accessed=10**6, transcendentals=0),
            name="smooth_and_mix",
        )(*windows, *sofar)

    result = add_beams([windows[0:1]] + [sent[h] for h in range(1, half)])
    result = add_beams([sent[half]], result)
    return add_beams([sent[h] for h in range(half + 1, bands)], result, last=True)


def solution(mesh):
    placed = (
        P("band", None, "tm"),
        P("band", None, None),
        P("band", None),
        P("band", "tm", None),
        P("band", "tm"),
        P("band", "tm"),
        P("band", None, None),
        P("band", None, None),
        P(None, "band", None),
    )
    return jax.shard_map(
        on_device,
        mesh=mesh,
        in_specs=placed,
        out_specs=P(None, "tm", "band", None),
        check_vma=False,
    )
```

```python
import functools

import jax
import jax.numpy as jnp
from jax import lax
from jax.experimental import pallas as pl
from jax.experimental.pallas import tpu as pltpu
from jax.sharding import PartitionSpec as P

L = 128
TROWS = 128
BLOCK = 256
VMEM = pl.BlockSpec(memory_space=pltpu.VMEM)
ANY = pl.BlockSpec(memory_space=pl.ANY)
SMALL = pltpu.CompilerParams(vmem_limit_bytes=32 * 2**20)
WHOLE = pltpu.CompilerParams(vmem_limit_bytes=48 * 2**20)
F32, BF16, FP8 = jnp.float32, jnp.bfloat16, jnp.float8_e4m3fn
TOP = 256.0
TINY = 1e-30


class Plan:
    def __init__(self, detectors, samples, taps):
        self.detectors, self.samples, self.taps = detectors, samples, taps
        self.groups = (taps - 1) // BLOCK
        self.steps = samples // BLOCK
        self.lead = self.groups - 1
        self.blocks = samples // L
        self.reach = (taps - 1) // 2 // L
        self.out = self.blocks + 2 * self.reach


def filter_kernel(
    weights_in, tod, taps_in, owner_in, row_in, counts_in,
    out, weights, taps, owner, tile_row, counts, held, held8, table, rest, table8, line, diagonal, sems, *, plan
):
    nd, steps, lead, groups = plan.detectors, plan.steps, plan.lead, plan.groups
    small = [
        pltpu.make_async_copy(src, dst, sems.at[steps + i])
        for i, (src, dst) in enumerate(
            ((taps_in.at[0], taps), (weights_in, weights), (owner_in, owner), (row_in, tile_row), (counts_in, counts))
        )
    ]
    big = [
        pltpu.make_async_copy(
            tod.at[0, :, b * BLOCK : (b + 1) * BLOCK], held.at[(lead + b) * nd : (lead + b + 1) * nd, :], sems.at[b]
        )
        for b in range(steps)
    ]
    for copy in small + big:
        copy.start()
    held[0 : lead * nd, :] = jnp.zeros((lead * nd, BLOCK), BF16)
    held[(lead + steps) * nd :, :] = jnp.zeros((lead * nd, BLOCK), BF16)
    held8[0 : lead * nd, :] = jnp.zeros((lead * nd, BLOCK), FP8)
    held8[(lead + steps) * nd :, :] = jnp.zeros((lead * nd, BLOCK), FP8)
    line[...] = jnp.zeros_like(line)
    row = lax.broadcasted_iota(jnp.int32, (nd, L), 0)
    lane = lax.broadcasted_iota(jnp.int32, (nd, L), 1)
    for copy in small:
        copy.wait()
    spread = jnp.broadcast_to(jnp.pad(weights[...], ((0, 0), (0, L - nd))), (nd, L))
    column = jnp.sum(jnp.where(row == lane, spread, 0.0), axis=1, keepdims=True)
    for pair in range(groups // 2):
        for half in range(2):
            parts = []
            for j in (2 * pair, 2 * pair + 1):
                start = j * BLOCK + half * L
                part = taps[:, start : start + L].astype(F32) * column
                parts.append(jnp.take_along_axis(part, L - 1 - lane, axis=1))
            turned = jnp.concatenate(parts, axis=0).T
            high = turned.astype(BF16)
            at = (1 - half) * L
            table[at : at + L, pair * L : (pair + 1) * L] = high
            rest[at : at + L, pair * L : (pair + 1) * L] = turned - high.astype(F32)
    left = jnp.maximum(jnp.max(jnp.abs(rest[...]), axis=0, keepdims=True), TINY)
    most = left[:, :nd]
    for j in range(1, groups):
        most = jnp.maximum(most, left[:, j * nd : (j + 1) * nd])
    table8[...] = (rest[...] * jnp.concatenate([TOP / most] * groups, axis=1)).astype(FP8)
    most = jnp.broadcast_to(jnp.pad(most, ((0, 0), (0, L - nd))), (nd, L))
    most = jnp.sum(jnp.where(row == lane, most, 0.0), axis=1, keepdims=True)
    last = jnp.broadcast_to(taps[:, groups * BLOCK : groups * BLOCK + 1].astype(F32) * column, (nd, L))
    row8 = lax.broadcasted_iota(jnp.int32, (8, L), 0)
    lane8 = lax.broadcasted_iota(jnp.int32, (8, L), 1)
    for copy in big:
        copy.wait()

    loud = jnp.zeros((nd, BLOCK), BF16)
    for b in range(steps):
        loud = jnp.maximum(loud, jnp.abs(held[(lead + b) * nd : (lead + b + 1) * nd, :]))
    loud = jnp.max(loud.astype(F32), axis=1, keepdims=True) * most
    largest = jnp.maximum(jnp.max(loud, axis=0, keepdims=True), TINY)
    quiet = jnp.broadcast_to(most * (TOP / largest), (nd, BLOCK))
    back = largest * (1.0 / (TOP * TOP))

    def shrink(b):
        if b < steps:
            at = (lead + b) * nd
            held8[at : at + nd, :] = (held[at : at + nd, :].astype(F32) * quiet).astype(FP8)

    slots = diagonal.shape[0]
    count = steps + lead

    def product(v):
        half = groups // 2
        low = half if v + half <= lead else 0
        high = half if v + half >= lead + steps else groups
        rows, cols = slice((v + low) * nd, (v + high) * nd), slice(low * nd, high * nd)
        main = jnp.dot(table[:, cols], held[rows, :], preferred_element_type=F32)
        small = jnp.dot(table8[:, cols], held8[rows, :], preferred_element_type=F32)
        diagonal[v % slots] = main + small * back

    def add_diagonals(tiles, at):
        total = direct = None
        for b in range(0, L, 8):
            part = tiles[0][b : b + 8]
            for other in tiles[1:]:
                part += other[b : b + 8]
            part = pltpu.roll(part, b + 1, 1, stride=1, stride_axis=0)
            kept = jnp.where(lane8 > row8 + b, part, 0.0)
            total = part if total is None else total + part
            direct = kept if direct is None else direct + kept
        line[at] += direct
        line[at + 1] += total - direct

    def corner(v, down, across):
        return diagonal[v % slots, down * L : (down + 1) * L, across * L : (across + 1) * L]

    shrink(0)
    shrink(1)
    product(0)
    for v in range(count):
        shrink(v + 2)
        if v + 1 < count:
            product(v + 1)
        first = [corner(v, 0, 0)] + ([corner(v - 1, 1, 1)] if v else [])
        add_diagonals(first, 2 * v)
        add_diagonals([corner(v, 1, 0), corner(v, 0, 1)], 2 * v + 1)
        if v >= lead:
            for half in range(2):
                x = held[v * nd : (v + 1) * nd, half * L : (half + 1) * L]
                line[2 * (v - lead) + half] += (x.astype(F32) * last).reshape(nd // 8, 8, L).sum(0)
    add_diagonals([corner(count - 1, 1, 1)], 2 * count)
    out[0 : plan.out, :] = jnp.sum(line[0 : plan.out], axis=1)

    nb = plan.blocks
    pad = ((0, 0), (0, L - nb))
    target = jnp.pad(owner[...], pad) * TROWS + jnp.pad(tile_row[...], pad)
    kept = lax.broadcasted_iota(jnp.int32, (1, L), 1) < counts[0, 0]
    target = jnp.where(kept, target, -1)
    out[plan.out : plan.out + 8, :] = jnp.broadcast_to(target.astype(F32), (8, L))


def two_terms(x):
    high = x.astype(BF16)
    return high, (x - high.astype(F32)).astype(BF16)


def rows_of(target, first, count):
    row = lax.broadcasted_iota(jnp.int32, (count, target.shape[1]), 0).astype(F32) + first
    row = jnp.where(row < 0, -2.0, row)
    return (jnp.broadcast_to(target, row.shape) == row).astype(BF16)


def add_rows(picks, blocks):
    high, low = two_terms(blocks)
    both = jnp.dot(picks, jnp.concatenate([high, low], axis=1), preferred_element_type=F32)
    return both[:, :L] + both[:, L:]


def tile_rows_kernel(*refs, plan, reach):
    parts, (home, away) = refs[:-2], refs[-2:]
    nb, halo = plan.blocks, plan.reach
    me = lax.axis_index("tm")
    ext = TROWS + 2 * reach
    marks_at = ext + 2 * halo * len(parts)
    away[marks_at:, :] = jnp.full((away.shape[0] - marks_at, L), -1.0, F32)

    for k, ref in enumerate(parts):
        at = ext + 2 * halo * k
        away[at : at + halo, :] = ref[0:halo, :]
        away[at + halo : at + 2 * halo, :] = ref[halo + nb : plan.out, :]
        away[marks_at + k : marks_at + k + 1, :] = ref[plan.out : plan.out + 1, :]
    target = jnp.concatenate([ref[plan.out : plan.out + 1, 0:nb] for ref in parts], axis=1)
    blocks = jnp.concatenate([ref[halo : halo + nb, :] for ref in parts], axis=0)
    for out, tile in ((home, me), (away, jnp.bitwise_xor(me, 1))):
        out[0:ext, :] = add_rows(rows_of(target, (tile * TROWS - reach).astype(F32), ext), blocks)


def windows_kernel(*refs, plan, order, bands, reach):
    home, here, other, beam_rows, beam_cols, mixing, out, marks, tile = refs
    me = lax.axis_index("tm")
    mine = lax.axis_index("band")
    nb, halo = plan.blocks, plan.reach
    ext = TROWS + 2 * reach
    after_rows = ext + 2 * halo * len(order)
    marks[...] = jnp.full_like(marks, -1.0)
    numbers = []
    for side, ref in enumerate((here, other)):
        for k, z in enumerate(order):
            t = jnp.bitwise_xor(me, 2 * z + side)
            marks[pl.ds(8 + t, 1), :] = ref[after_rows + k : after_rows + k + 1, :]
            numbers.append(t)
    targets = []
    for t in numbers:
        before = marks[pl.ds(7 + t, 1), :]
        after = marks[pl.ds(9 + t, 1), :]
        targets += [before[:, nb - halo : nb], after[:, 0:halo]]
    blocks = [here[ext:after_rows, :], other[ext:after_rows, :]]
    picks = rows_of(jnp.concatenate(targets, axis=1), (me * TROWS - reach).astype(F32), ext)
    tile[...] = home[...] + other[0:ext, :] + add_rows(picks, jnp.concatenate(blocks, axis=0))
    share = TROWS // bands
    wide = share + 2 * reach
    terms, taps = beam_rows.shape[1:]
    comps = mixing.shape[0]
    out[...] = jnp.zeros_like(out)
    pad = jnp.zeros((8, L - taps), F32)
    lane = lax.broadcasted_iota(jnp.int32, (8, L), 1)
    turn = jnp.where(lane < taps, taps - 1 - lane, lane)
    for h in range(bands):
        start = pl.multiple_of(jnp.bitwise_xor(mine, h) * share, 8)
        out[h, 0:wide, :] = tile[pl.ds(start, wide), :]
        for k in range(terms):
            out[h, wide + k : wide + k + 1, 0:taps] = beam_rows[0, k : k + 1, :]
            profile = jnp.broadcast_to(beam_cols[0, k : k + 1, :], (8, taps))
            turned = jnp.take_along_axis(jnp.concatenate([profile, pad], axis=1), turn, axis=1)
            out[h, wide + terms + k : wide + terms + k + 1, :] = turned[0:1]
        for c in range(comps):
            at = wide + 2 * terms
            out[h, at : at + 1, c * terms : (c + 1) * terms] = mixing[c, 0:1, :]


def dot3(a, b, dims):
    a0, a1 = two_terms(a)
    b0, b1 = two_terms(b)
    ka, kb = dims
    left = jnp.concatenate([a0, a0, a1], axis=ka)
    right = jnp.concatenate([b0, b1, b0], axis=kb)
    return lax.dot_general(left, right, (((ka,), (kb,)), ((), ())), preferred_element_type=F32)


def beam_kernel(*refs, windows, share, reach, terms, comps):
    ins, sofar, out = refs[:windows], refs[windows:-1], refs[-1]
    wide = share + 2 * reach
    x = lax.broadcasted_iota(jnp.int32, (L, L), 0)
    c_in = lax.broadcasted_iota(jnp.int32, (L, L), 1)
    near = jnp.abs(c_in - x) <= reach
    totals = [sofar[0][c, 0] if sofar else None for c in range(comps)]
    for ref in ins:
        for h in range(ref.shape[0]):
            rows = ref[h, 0:wide, :]
            mats = []
            for k in range(terms):
                spread = jnp.broadcast_to(ref[h, wide + k : wide + k + 1, :], (share, L))
                mats.append(pltpu.roll(spread, 0, 1, stride=1, stride_axis=0)[:, :wide])
            rowed = dot3(jnp.concatenate(mats, axis=0), rows, (1, 0))
            for k in range(terms):
                at = wide + terms + k
                spread = jnp.broadcast_to(ref[h, at : at + 1, :], (L, L))
                cols = pltpu.roll(spread, L - reach, 1, stride=1, stride_axis=0)
                cols = jnp.where(near, cols, 0.0)
                beamed = dot3(rowed[k * share : (k + 1) * share], cols, (1, 0))
                for c in range(comps):
                    at, lane = wide + 2 * terms, c * terms + k
                    part = beamed * ref[h, at : at + 1, lane : lane + 1]
                    totals[c] = part if totals[c] is None else totals[c] + part
    for c in range(comps):
        out[c, 0] = totals[c]


def flip(x, axis, bits):
    count = lax.axis_size(axis)
    return lax.ppermute(x, axis, [(i, i ^ bits) for i in range(count)])


def on_device(
    tod, filter_taps, det_weights, owner, tile_row, block_counts, beam_rows, beam_cols, mixing
):
    detectors, samples = tod.shape[1:]
    taps = filter_taps.shape[2]
    plan = Plan(detectors, samples, taps)
    tms, bands = lax.axis_size("tm"), lax.axis_size("band")
    inner = 2
    outer = tms // inner
    terms, beam = beam_rows.shape[1:]
    reach = (beam - 1) // 2
    comps = mixing.shape[0]
    inputs = (det_weights, tod, filter_taps, owner[:, :, 0], tile_row)
    values = pl.pallas_call(
        functools.partial(filter_kernel, plan=plan),
        out_shape=jax.ShapeDtypeStruct((plan.out + 8, L), F32),
        in_specs=[ANY] * 6,
        out_specs=VMEM,
        scratch_shapes=[
            pltpu.VMEM((1, detectors), F32),
            pltpu.VMEM((detectors, taps), BF16),
            pltpu.VMEM((1, plan.blocks), jnp.int32),
            pltpu.VMEM((1, plan.blocks), jnp.int32),
            pltpu.SMEM((1, 1), jnp.int32),
            pltpu.VMEM(((plan.steps + 2 * plan.lead) * detectors, BLOCK), BF16),
            pltpu.VMEM(((plan.steps + 2 * plan.lead) * detectors, BLOCK), FP8),
            pltpu.VMEM((BLOCK, plan.groups * detectors), BF16),
            pltpu.VMEM((BLOCK, plan.groups * detectors), F32),
            pltpu.VMEM((BLOCK, plan.groups * detectors), FP8),
            pltpu.VMEM((plan.out + 8, 8, L), F32),
            pltpu.VMEM((3, BLOCK, BLOCK), F32),
            pltpu.SemaphoreType.DMA((plan.steps + 5,)),
        ],
        compiler_params=WHOLE,
        name="filter_blocks",
    )(*[pltpu.with_memory_space_constraint(v, pltpu.HBM) for v in inputs], block_counts)
    order = list(range(outer))
    parts = [flip(values, "tm", k * inner) if k else values for k in order]
    ext = TROWS + 2 * reach
    sent = ext + 2 * plan.reach * outer + -(-outer // 8) * 8
    home, away = pl.pallas_call(
        functools.partial(tile_rows_kernel, plan=plan, reach=reach),
        out_shape=(jax.ShapeDtypeStruct((ext, L), F32), jax.ShapeDtypeStruct((sent, L), F32)),
        in_specs=[VMEM] * outer,
        out_specs=(VMEM, VMEM),
        compiler_params=SMALL,
        name="tile_rows",
    )(*parts)
    other = flip(away, "tm", 1)
    share = TROWS // bands
    wide = share + 2 * reach
    extra = -(-(2 * terms + 1) // 8) * 8
    windows = pl.pallas_call(
        functools.partial(windows_kernel, plan=plan, order=order, bands=bands, reach=reach),
        out_shape=jax.ShapeDtypeStruct((bands, wide + extra, L), F32),
        in_specs=[VMEM] * 6,
        out_specs=VMEM,
        scratch_shapes=[pltpu.VMEM((16 + tms, L), F32), pltpu.VMEM((ext, L), F32)],
        compiler_params=SMALL,
        name="band_windows",
    )(home, away, other, beam_rows, beam_cols, mixing)
    half = bands // 2
    sent = {h: flip(windows[h : h + 1], "band", h) for h in list(range(half, bands)) + list(range(1, half))}
    smooth = functools.partial(beam_kernel, share=share, reach=reach, terms=terms, comps=comps)

    def add_beams(windows, *sofar):
        return pl.pallas_call(
            functools.partial(smooth, windows=len(windows)),
            out_shape=jax.ShapeDtypeStruct((comps, 1, share, L), F32),
            in_specs=[VMEM] * (len(windows) + len(sofar)),
            out_specs=VMEM,
            compiler_params=SMALL,
            cost_estimate=pl.CostEstimate(flops=10**9, bytes_accessed=10**6, transcendentals=0),
            name="smooth_and_mix",
        )(*windows, *sofar)

    result = add_beams([windows[0:1]] + [sent[h] for h in range(1, half)])
    result = add_beams([sent[half]], result)
    return add_beams([sent[h] for h in range(half + 1, bands)], result)


def solution(mesh):
    placed = (
        P("band", None, "tm"),
        P("band", None, None),
        P("band", None),
        P("band", "tm", None),
        P("band", "tm"),
        P("band", "tm"),
        P("band", None, None),
        P("band", None, None),
        P(None, "band", None),
    )
    return jax.shard_map(
        on_device,
        mesh=mesh,
        in_specs=placed,
        out_specs=P(None, "tm", "band", None),
        check_vma=False,
    )
```
